128 devices in a mesh: dp: 128 (over y, x, z, core).
Axes of the slice: x: 4, y: 4, z: 4, core: 2. Of those that a mesh axis runs over, the one named last changes fastest.
Arguments:
- teacher: bfloat16 [128, 128, 1536], P('dp'), may hold values from -24 to 24
- head_weight: bfloat16 [1536, 384], replicated, may hold values from -0.15625 to 0.15625
- neighbours: int32 [128, 6], replicated, may hold values from 0 to 127, as said below
Outputs:
- head_grad: float32 [1536, 384], P('dp')
- code_grad: float32 [128, 128, 384], P('dp')
The draws below stay inside these ranges and needn't reach their ends.
Inputs may be any that keep to these rules, and one draw needn't show every extreme that they name: `neighbours`: each row names 6 different images, never its own index.
All inputs are finite; a program needn't handle non-finite values.
Results may differ from the reference program's by a relative error of at most 0.015.
Values may be sent and summed in bfloat16 or wider, within the bound.
A program may use at most 64 MiB of HBM per device.

```python
import jax
import jax.numpy as jnp
from jax import lax

D = 1536
K = 384
PATCHES = 128
KNN = 6
IMAGES = 128


def draw_neighbours(key, part):
    key = jax.random.fold_in(key, 11)
    key_pick, key_boost, key_score = jax.random.split(key, 3)
    popular = jax.random.randint(key_pick, (IMAGES,), 0, 4) == 0
    boost = jax.random.randint(key_boost, (IMAGES,), 0, 16384) * popular.astype(jnp.int32)
    scores = jax.random.randint(key_score, (IMAGES, IMAGES), 0, 16384) + boost[None, :]
    rowids = lax.broadcasted_iota(jnp.int32, (IMAGES, IMAGES), 0)
    colids = lax.broadcasted_iota(jnp.int32, (IMAGES, IMAGES), 1)
    scores = jnp.where(rowids == colids, -1, scores)
    distinct = scores * IMAGES + colids
    _, picked = lax.top_k(distinct, KNN)
    return picked.astype(jnp.int32)


def raised(result, rng, source, target, parts, factor):
    owner, partner = [(jnp.arange(result.shape[position]) // (result.shape[position] // parts)).reshape([-1 if axis == position else 1 for axis in range(result.ndim)]) for position in (source, target)]
    chosen = jax.random.permutation(rng, parts)[partner]
    strong = (owner == chosen) | (owner == (partner + parts // 2) % parts)
    return jnp.where(strong, factor * result, result)


def levels(stream_key, extent, shards, least, high):
    loudness, own = 1.0, jax.random.fold_in(stream_key, 6)
    for dim, blocks in shards:
        steps = jnp.exp(jax.random.uniform(jax.random.fold_in(own, dim), (blocks,), jnp.float32, least / len(shards), high / len(shards)))
        loudness = loudness * jnp.repeat(steps, extent[dim] // blocks).reshape([-1 if axis == dim else 1 for axis in range(len(extent))])
    return loudness


def scatter_about(key, dims, width, limit, pieces=(), kind=jnp.bfloat16):
    factor_of = levels(key, dims, pieces, -0.22, 0.18) if pieces else 1.0
    entries = jax.random.normal(key, dims, jnp.float32) * width * factor_of
    return jnp.minimum(jnp.maximum(entries, -limit), limit).astype(kind)


def gaussian_with(rng, dims, spread, bound, cuts, heavy, held_as=jnp.bfloat16):
    entries = spread * jax.random.normal(rng, dims, jnp.float32)
    if cuts:
        entries = entries * levels(rng, dims, cuts, -0.22, 0.18)
    return jnp.clip(raised(entries, jax.random.fold_in(rng, 3), *heavy), -bound, bound).astype(held_as)


def setup_inputs(seed: int = 0) -> dict:
    streams_of = jax.random.split(jax.random.key(seed), 4)
    teacher = gaussian_with(streams_of[0], (IMAGES, PATCHES, D), 1.0, 24.0, ((0, 128),), (0, 2, 128, 5.5))
    head_weight = scatter_about(streams_of[1], (D, K), D ** -0.5, 0.15625)
    neighbours = draw_neighbours(jax.random.fold_in(streams_of[3], 71), 0)
    return dict(teacher=teacher, head_weight=head_weight, neighbours=neighbours)


EPS = 1e-06
LOSS_SCALE = 128.0
SHIFT_SELF = 0.18
WEIGHT_SELF = 0.1
SHIFT_PAIR = 0.12
WEIGHT_PAIR = 0.5

def unit_rows(features):
    values = features.astype(jnp.float32)
    return values * lax.rsqrt(lax.optimization_barrier(jnp.sum(values * values, axis=-1, keepdims=True)) + EPS)

def gate_tile(unit_a, unit_b, code_a, code_b, shift, weight):
    tcorr = jnp.dot(unit_a, unit_b.T, preferred_element_type=jnp.float32)
    scor = jnp.dot(code_a, code_b.T, preferred_element_type=jnp.float32)
    return (-(LOSS_SCALE * weight) * (tcorr - shift) * jnp.maximum(scor, 0.0)).astype(jnp.bfloat16)

def back_norm(grad, code_unit, inverse):
    values = code_unit.astype(jnp.float32)
    return (grad - values * lax.optimization_barrier(jnp.sum(values * grad, axis=-1, keepdims=True))) * inverse

def reference(teacher, head_weight, neighbours):
    units = unit_rows(teacher).astype(jnp.bfloat16)
    codes = lax.map(lambda block: jnp.dot(block, head_weight, preferred_element_type=jnp.float32).astype(jnp.bfloat16), units)
    code_vals = codes.astype(jnp.float32)
    inverses = lax.rsqrt(lax.optimization_barrier(jnp.sum(code_vals * code_vals, axis=-1, keepdims=True)) + EPS)
    code_units = (code_vals * inverses).astype(jnp.bfloat16)

    def step(incoming, index):
        unit_a = units[index]
        code_a = code_units[index]
        gate_self = gate_tile(unit_a, unit_a, code_a, code_a, SHIFT_SELF, WEIGHT_SELF)
        grad = jnp.dot(gate_self, code_a, preferred_element_type=jnp.float32)
        grad = grad + jnp.dot(gate_self.T, code_a, preferred_element_type=jnp.float32)
        for slot in range(KNN):
            partner = neighbours[index, slot]
            unit_b = units[partner]
            code_b = code_units[partner]
            gate_pair = gate_tile(unit_a, unit_b, code_a, code_b, SHIFT_PAIR, WEIGHT_PAIR)
            grad = grad + jnp.dot(gate_pair, code_b, preferred_element_type=jnp.float32)
            cross_raw = jnp.dot(gate_pair.T, code_a, preferred_element_type=jnp.float32)
            cross = back_norm(cross_raw, code_b, inverses[partner]).astype(jnp.bfloat16)
            incoming = incoming.at[partner].add(cross.astype(jnp.float32))
        own = back_norm(grad, code_a, inverses[index])
        return (incoming, own)
    start = jnp.zeros((IMAGES, PATCHES, K), jnp.float32)
    incoming, owns = lax.scan(step, start, jnp.arange(IMAGES, dtype=jnp.int32))
    relayed = lax.optimization_barrier(incoming.astype(jnp.bfloat16))
    code_grad = owns + relayed.astype(jnp.float32)
    code_half = code_grad.astype(jnp.bfloat16)

    def accumulate(total, index):
        return (total + jnp.dot(units[index].T, code_half[index], preferred_element_type=jnp.float32), None)
    head_grad, _ = lax.scan(accumulate, jnp.zeros((D, K), jnp.float32), jnp.arange(IMAGES, dtype=jnp.int32))
    return (head_grad, code_grad)
```

```python
import jax
import jax.numpy as jnp
from jax import lax
from jax.sharding import PartitionSpec as P

EPS = 1e-06
LOSS_SCALE = 128.0
SHIFT_SELF = 0.18
WEIGHT_SELF = 0.1
SHIFT_PAIR = 0.12
WEIGHT_PAIR = 0.5


def unit_rows(features):
    values = features.astype(jnp.float32)
    return values * lax.rsqrt(jnp.sum(values * values, axis=-1, keepdims=True) + EPS)


def code_scale(codes):
    values = codes.astype(jnp.float32)
    return lax.rsqrt(jnp.sum(values * values, axis=-1, keepdims=True) + EPS)


def back_norm(grad, code_unit, inverse):
    values = code_unit.astype(jnp.float32)
    return (grad - values * jnp.sum(values * grad, axis=-1, keepdims=True)) * inverse


def body(teacher, head_weight, neighbours):
    count = lax.axis_size("dp")
    patches = teacher.shape[1]
    width = teacher.shape[2]
    code_width = head_weight.shape[1]
    rows = patches // count
    images = neighbours.shape[0]
    slots = neighbours.shape[1]
    own_unit = unit_rows(teacher[0]).astype(jnp.bfloat16)
    codes = jnp.dot(own_unit, head_weight, preferred_element_type=jnp.float32).astype(jnp.bfloat16)
    own_inv = code_scale(codes)
    own_code = (codes.astype(jnp.float32) * own_inv).astype(jnp.bfloat16)
    unit_pieces = own_unit.reshape(count, rows, width)
    held_units = lax.all_to_all(unit_pieces, "dp", split_axis=0, concat_axis=0, tiled=True)
    order = jnp.transpose(neighbours)
    send_units = held_units[order]
    tcorr_self = jnp.einsum("pd,qd->pq", own_unit, own_unit, preferred_element_type=jnp.float32)
    scor_self = jnp.einsum("pc,qc->pq", own_code, own_code, preferred_element_type=jnp.float32)
    gate_self = (
        -(LOSS_SCALE * WEIGHT_SELF) * (tcorr_self - SHIFT_SELF) * jnp.maximum(scor_self, 0.0)
    ).astype(jnp.bfloat16)
    grad_self = jnp.einsum("pq,qc->pc", gate_self, own_code, preferred_element_type=jnp.float32)
    grad_self = grad_self + jnp.einsum(
        "qp,qc->pc", gate_self, own_code, preferred_element_type=jnp.float32
    )
    partner_units = lax.all_to_all(send_units, "dp", split_axis=1, concat_axis=1, tiled=True)
    items = partner_units.shape[0]
    finish_partner_units = partner_units.reshape(items, patches, width)
    finish_partner_codes = jnp.einsum(
        "nqd,dc->nqc", finish_partner_units, head_weight, preferred_element_type=jnp.float32
    ).astype(jnp.bfloat16)
    partner_inv = code_scale(finish_partner_codes)
    partner_code = (finish_partner_codes.astype(jnp.float32) * partner_inv).astype(jnp.bfloat16)
    tcorr = jnp.einsum(
        "pd,nqd->npq", own_unit, finish_partner_units, preferred_element_type=jnp.float32
    )
    scor = jnp.einsum("pc,nqc->npq", own_code, partner_code, preferred_element_type=jnp.float32)
    gate = (-(LOSS_SCALE * WEIGHT_PAIR) * (tcorr - SHIFT_PAIR) * jnp.maximum(scor, 0.0)).astype(
        jnp.bfloat16
    )
    grads = jnp.einsum("npq,nqc->npc", gate, partner_code, preferred_element_type=jnp.float32)
    cross_raw = jnp.einsum("npq,pc->nqc", gate, own_code, preferred_element_type=jnp.float32)
    cross = back_norm(cross_raw, partner_code, partner_inv).astype(jnp.bfloat16)
    grads, cross = (grads, cross)
    grad_total = grad_self + jnp.sum(grads, axis=0)
    own_grad = back_norm(grad_total, own_code, own_inv)
    arrived = lax.all_to_all(
        cross.reshape(slots, count, rows, code_width), "dp", split_axis=1, concat_axis=1, tiled=True
    )
    targets = lax.broadcasted_iota(jnp.int32, (images, slots, images), 0)
    member = (order[None, :, :] == targets).astype(jnp.bfloat16)
    relayed = jnp.einsum(
        "jki,kirc->jrc", member, arrived, preferred_element_type=jnp.float32
    ).astype(jnp.bfloat16)
    collected = lax.all_to_all(relayed, "dp", split_axis=0, concat_axis=0, tiled=True)
    code_grad = own_grad + collected.reshape(patches, code_width).astype(jnp.float32)
    code_half = code_grad.astype(jnp.bfloat16)
    partial_grad = jnp.einsum("pd,pc->dc", own_unit, code_half, preferred_element_type=jnp.float32)
    shares = partial_grad.astype(jnp.bfloat16).reshape(count, width // count, code_width)
    arrived_shares = lax.all_to_all(shares, "dp", split_axis=0, concat_axis=0, tiled=True)
    head_grad = jnp.sum(arrived_shares.astype(jnp.float32), axis=0)
    return (head_grad, code_grad[None])


def solution(mesh):
    return jax.shard_map(
        body,
        mesh=mesh,
        in_specs=(P("dp", None, None), P(), P()),
        out_specs=(P("dp", None), P("dp", None, None)),
        check_vma=False,
    )
```

```python
import functools

import jax
import jax.numpy as jnp
from jax import lax
from jax.experimental import pallas as pl
from jax.experimental.pallas import tpu as pltpu
from jax.sharding import PartitionSpec as P

EPS = 1e-06
LOSS_SCALE = 128.0
SHIFT_SELF = 0.18
WEIGHT_SELF = 0.1
SHIFT_PAIR = 0.12
WEIGHT_PAIR = 0.5
MESH = pl.DeviceIdType.MESH
SIDE = 4
RING = 32
KNN = 6


def place(orient, index):
    y, x, z, c = index >> 5, (index >> 3) & 3, (index >> 1) & 3, index & 1
    if orient == 0:
        return y, index & 31
    if orient == 1:
        return x, (y << 3) + (index & 7)
    return z, ((index >> 3) << 1) + c


def device_at(orient, layer, spot):
    if orient == 0:
        return (layer << 5) + spot
    if orient == 1:
        return ((spot >> 3) << 5) + (layer << 3) + (spot & 7)
    return ((spot >> 1) << 3) + (layer << 1) + (spot & 1)


def shifted(spot, step):
    a = ((spot >> 3) + (step >> 3)) & 3
    b = ((spot >> 1) + (step >> 1)) & 3
    return (a << 3) + (b << 1) + ((spot + step) & 1)


def remote(src, dst, send, recv, device):
    return pltpu.make_async_remote_copy(
        src_ref=src, dst_ref=dst, send_sem=send, recv_sem=recv, device_id=(device,), device_id_type=MESH
    )


def front(nb_ref, teacher_ref, unit_ref, partner_ref, held0, held1, held2, picked, own_sem, send1, recv1, send2, recv2, send3, recv3):
    held = (held0, held1, held2)
    me = lax.axis_index("dp")
    where = [place(o, me) for o in range(3)]
    barrier = pltpu.get_barrier_semaphore()

    def greet(step, carry):
        for o in range(3):
            layer, spot = where[o]
            pl.semaphore_signal(barrier, inc=1, device_id=(device_at(o, layer, shifted(spot, step)),), device_id_type=MESH)
        return carry

    lax.fori_loop(1, RING, greet, 0)
    values = teacher_ref[0].astype(jnp.float32)
    total = jnp.sum(values * values, axis=-1, keepdims=True)
    unit_ref[...] = (values * lax.rsqrt(total + EPS)).astype(jnp.bfloat16)
    pl.semaphore_wait(barrier, 3 * (RING - 1))

    def tile(ref, o, spot):
        rows = pl.ds(pl.multiple_of((spot >> 2) * 16, 16), 16)
        cols = pl.ds(pl.multiple_of(512 * o + (spot & 3) * 128, 128), 128)
        return ref.at[rows, cols]

    def deal(step, carry):
        for o in range(3):
            layer, spot = where[o]
            target = shifted(spot, step)
            remote(
                tile(unit_ref, o, target), held[o].at[layer * RING + spot], send1.at[o], recv1.at[o],
                device_at(o, layer, target),
            ).start()
        return carry

    own = []
    for o in range(3):
        layer, spot = where[o]
        own.append(pltpu.make_async_copy(tile(unit_ref, o, spot), held[o].at[layer * RING + spot], own_sem.at[o]))
        own[o].start()
    lax.fori_loop(1, RING, deal, 0)
    for o in range(3):
        layer, spot = where[o]
        own[o].wait()
        part = held[o].at[pl.ds(0, RING - 1)]
        remote(part, part, send1.at[o], recv1.at[o], me).wait()
        mine = held[o].at[pl.ds(layer * RING, RING)]
        for hop in range(1, SIDE):
            remote(mine, mine, send2.at[o], recv2.at[o], device_at(o, (layer + hop) & 3, spot)).start()

    for o in range(3):
        layer, spot = where[o]
        part = held[o].at[pl.ds(0, RING * (SIDE - 1))]
        remote(part, part, send2.at[o], recv2.at[o], me).wait()
    rows_of = [(pl.ds(pl.multiple_of((where[o][1] >> 2) * 16, 16), 16),
                pl.ds(pl.multiple_of(512 * o + (where[o][1] & 3) * 128, 128), 128)) for o in range(3)]

    def pick(o, step):
        layer, spot = where[o]
        asker = device_at(o, layer, shifted(spot, step))
        for k in range(KNN):
            up, at = place(o, nb_ref[k, asker])
            picked[o, step, k] = held[o][(up << 5) + at]
        return asker

    for o in range(3):
        pick(o, 0)
        pltpu.make_async_copy(picked.at[o, 0], partner_ref.at[:, rows_of[o][0], rows_of[o][1]], own_sem.at[o]).start()

    def serve(step, carry):
        for o in range(3):
            asker = pick(o, step)
            remote(
                picked.at[o, step], partner_ref.at[:, rows_of[o][0], rows_of[o][1]], send3.at[o], recv3.at[o], asker
            ).start()
        return carry

    lax.fori_loop(1, RING, serve, 0)
    for o in range(3):
        pltpu.make_async_copy(picked.at[o, 0], picked.at[o, 0], own_sem.at[o]).wait()
        part = picked.at[o, pl.ds(1, RING - 1)]
        remote(part, part, send3.at[o], recv3.at[o], me).wait()


def fetch(teacher, neighbours):
    smem = pl.BlockSpec(memory_space=pltpu.SMEM)
    vmem = pl.BlockSpec(memory_space=pltpu.VMEM)
    return pl.pallas_call(
        front,
        out_shape=(
            jax.ShapeDtypeStruct((128, 1536), jnp.bfloat16),
            jax.ShapeDtypeStruct((KNN, 128, 1536), jnp.bfloat16),
        ),
        in_specs=[smem, vmem],
        out_specs=(vmem, vmem),
        scratch_shapes=[pltpu.VMEM((128, 16, 128), jnp.bfloat16)] * 3
        + [pltpu.VMEM((3, RING, KNN, 16, 128), jnp.bfloat16)]
        + [pltpu.SemaphoreType.DMA((3,))] * 7,
        compiler_params=pltpu.CompilerParams(
            collective_id=0, has_side_effects=True, vmem_limit_bytes=32 * 2**20
        ),
    )(jnp.transpose(neighbours), teacher)


def code_scale(codes):
    values = codes.astype(jnp.float32)
    return lax.rsqrt(jnp.sum(values * values, axis=-1, keepdims=True) + EPS)


def back_norm(grad, code_unit, inverse):
    values = code_unit.astype(jnp.float32)
    return (grad - values * jnp.sum(values * grad, axis=-1, keepdims=True)) * inverse


def body(teacher, head_weight, neighbours):
    count = lax.axis_size("dp")
    patches = teacher.shape[1]
    width = teacher.shape[2]
    code_width = head_weight.shape[1]
    rows = patches // count
    images = neighbours.shape[0]
    slots = neighbours.shape[1]
    own_unit, partner_units = fetch(teacher, neighbours)
    codes = jnp.dot(own_unit, head_weight, preferred_element_type=jnp.float32).astype(jnp.bfloat16)
    own_inv = code_scale(codes)
    own_code = (codes.astype(jnp.float32) * own_inv).astype(jnp.bfloat16)
    order = jnp.transpose(neighbours)
    tcorr_self = jnp.einsum("pd,qd->pq", own_unit, own_unit, preferred_element_type=jnp.float32)
    scor_self = jnp.einsum("pc,qc->pq", own_code, own_code, preferred_element_type=jnp.float32)
    gate_self = (
        -(LOSS_SCALE * WEIGHT_SELF) * (tcorr_self - SHIFT_SELF) * jnp.maximum(scor_self, 0.0)
    ).astype(jnp.bfloat16)
    grad_self = jnp.einsum("pq,qc->pc", gate_self, own_code, preferred_element_type=jnp.float32)
    grad_self = grad_self + jnp.einsum(
        "qp,qc->pc", gate_self, own_code, preferred_element_type=jnp.float32
    )
    finish_partner_codes = jnp.einsum(
        "nqd,dc->nqc", partner_units, head_weight, preferred_element_type=jnp.float32
    ).astype(jnp.bfloat16)
    partner_inv = code_scale(finish_partner_codes)
    partner_code = (finish_partner_codes.astype(jnp.float32) * partner_inv).astype(jnp.bfloat16)
    tcorr = jnp.einsum(
        "pd,nqd->npq", own_unit, partner_units, preferred_element_type=jnp.float32
    )
    scor = jnp.einsum("pc,nqc->npq", own_code, partner_code, preferred_element_type=jnp.float32)
    gate = (-(LOSS_SCALE * WEIGHT_PAIR) * (tcorr - SHIFT_PAIR) * jnp.maximum(scor, 0.0)).astype(
        jnp.bfloat16
    )
    grads = jnp.einsum("npq,nqc->npc", gate, partner_code, preferred_element_type=jnp.float32)
    cross_raw = jnp.einsum("npq,pc->nqc", gate, own_code, preferred_element_type=jnp.float32)
    cross = back_norm(cross_raw, partner_code, partner_inv).astype(jnp.bfloat16)
    grad_total = grad_self + jnp.sum(grads, axis=0)
    own_grad = back_norm(grad_total, own_code, own_inv)
    arrived = lax.all_to_all(
        cross.reshape(slots, count, rows, code_width), "dp", split_axis=1, concat_axis=1, tiled=True
    )
    targets = lax.broadcasted_iota(jnp.int32, (images, slots, images), 0)
    member = (order[None, :, :] == targets).astype(jnp.bfloat16)
    relayed = jnp.einsum(
        "jki,kirc->jrc", member, arrived, preferred_element_type=jnp.float32
    ).astype(jnp.bfloat16)
    collected = lax.all_to_all(relayed, "dp", split_axis=0, concat_axis=0, tiled=True)
    code_grad = own_grad + collected.reshape(patches, code_width).astype(jnp.float32)
    code_half = code_grad.astype(jnp.bfloat16)
    partial_grad = jnp.einsum("pd,pc->dc", own_unit, code_half, preferred_element_type=jnp.float32)
    shares = partial_grad.astype(jnp.bfloat16).reshape(count, width // count, code_width)
    arrived_shares = lax.all_to_all(shares, "dp", split_axis=0, concat_axis=0, tiled=True)
    head_grad = jnp.sum(arrived_shares.astype(jnp.float32), axis=0)
    return (head_grad, code_grad[None])


def solution(mesh):
    return jax.shard_map(
        body,
        mesh=mesh,
        in_specs=(P("dp", None, None), P(), P()),
        out_specs=(P("dp", None), P("dp", None, None)),
        check_vma=False,
    )
```

```python
import jax
import jax.numpy as jnp
from jax import lax
from jax.experimental import pallas as pl
from jax.experimental.pallas import tpu as pltpu
from jax.sharding import PartitionSpec as P

EPS = 1e-06
LOSS_SCALE = 128.0
SHIFT_SELF = 0.18
WEIGHT_SELF = 0.1
SHIFT_PAIR = 0.12
WEIGHT_PAIR = 0.5
MESH = pl.DeviceIdType.MESH
SIDE = 4
RING = 32
KNN = 6


def place(orient, index):
    y, x, z, c = index >> 5, (index >> 3) & 3, (index >> 1) & 3, index & 1
    if orient == 0:
        return y, index & 31
    if orient == 1:
        return x, (y << 3) + (index & 7)
    return z, ((index >> 3) << 1) + c


def device_at(orient, layer, spot):
    if orient == 0:
        return (layer << 5) + spot
    if orient == 1:
        return ((spot >> 3) << 5) + (layer << 3) + (spot & 7)
    return ((spot >> 1) << 3) + (layer << 1) + (spot & 1)


def shifted(spot, step):
    a = ((spot >> 3) + (step >> 3)) & 3
    b = ((spot >> 1) + (step >> 1)) & 3
    return (a << 3) + (b << 1) + ((spot + step) & 1)


def remote(src, dst, send, recv, device):
    return pltpu.make_async_remote_copy(
        src_ref=src, dst_ref=dst, send_sem=send, recv_sem=recv, device_id=(device,), device_id_type=MESH
    )


def unit_rows(values):
    total = jnp.sum(values * values, axis=-1, keepdims=True)
    return (values * lax.rsqrt(total + EPS)).astype(jnp.bfloat16)


def code_rows(codes):
    values = codes.astype(jnp.bfloat16).astype(jnp.float32)
    inverse = lax.rsqrt(jnp.sum(values * values, axis=-1, keepdims=True) + EPS)
    return (values * inverse).astype(jnp.bfloat16), inverse


def back_norm(grad, code_unit, inverse):
    values = code_unit.astype(jnp.float32)
    return (grad - values * jnp.sum(values * grad, axis=-1, keepdims=True)) * inverse


def dot(a, b, dims=((1,), (0,))):
    return lax.dot_general(a, b, (dims, ((), ())), preferred_element_type=jnp.float32)


def step_kernel(
    nb_ref, nbv_ref, teacher_hbm, weight_hbm, head_ref, grad_ref,
    teacher_ref, weight_ref, unit_ref, code_ref, inv_ref, self_ref, tall_ref, tallp_ref, perm_ref, member_ref,
    held0, held1, held2, picked, partner_ref, cross_out, cross_in, back_out, back_mid, back_in,
    share_out, share_mid, share_sum, share_in,
    load_sem, own_sem, send1, recv1, send2, recv2, send3, recv3, send4, recv4,
):
    held = (held0, held1, held2)
    me = lax.axis_index("dp")
    where = [place(o, me) for o in range(3)]
    column, lane = me >> 3, me & 7
    chip, core = me >> 1, me & 1
    barrier = pltpu.get_barrier_semaphore()
    loads = [
        pltpu.make_async_copy(teacher_hbm.at[0], teacher_ref, load_sem.at[0]),
        pltpu.make_async_copy(weight_hbm, weight_ref, load_sem.at[1]),
    ]
    for load in loads:
        load.start()

    def greet(step, carry):
        for o in range(3):
            layer, spot = where[o]
            pl.semaphore_signal(barrier, inc=1, device_id=(device_at(o, layer, shifted(spot, step)),), device_id_type=MESH)
        return carry

    lax.fori_loop(1, RING, greet, 0)
    loads[0].wait()
    unit_ref[...] = unit_rows(teacher_ref[...].astype(jnp.float32))
    pl.semaphore_wait(barrier, 3 * (RING - 1))

    def tile(ref, o, spot):
        rows = pl.ds(pl.multiple_of((spot >> 2) * 16, 16), 16)
        cols = pl.ds(pl.multiple_of(512 * o + (spot & 3) * 128, 128), 128)
        return ref.at[rows, cols]

    def deal(step, carry):
        for o in range(3):
            layer, spot = where[o]
            target = shifted(spot, step)
            remote(
                tile(unit_ref, o, target), held[o].at[layer * RING + spot], send1.at[o], recv1.at[o],
                device_at(o, layer, target),
            ).start()
        return carry

    own = []
    for o in range(3):
        layer, spot = where[o]
        own.append(pltpu.make_async_copy(tile(unit_ref, o, spot), held[o].at[layer * RING + spot], own_sem.at[o]))
        own[o].start()
    lax.fori_loop(1, RING, deal, 0)

    loads[1].wait()
    code_unit, inverse = code_rows(dot(unit_ref[...], weight_ref[...]))
    code_ref[...] = code_unit
    inv_ref[...] = jnp.broadcast_to(inverse, inv_ref.shape)

    for o in range(3):
        layer, spot = where[o]
        own[o].wait()
        part = held[o].at[pl.ds(0, RING - 1)]
        remote(part, part, send1.at[o], recv1.at[o], me).wait()
        mine = held[o].at[pl.ds(layer * RING, RING)]
        for hop in range(1, SIDE):
            remote(mine, mine, send2.at[o], recv2.at[o], device_at(o, (layer + hop) & 3, spot)).start()

    units, codes = unit_ref[...], code_ref[...]
    tcorr = dot(units, units, ((1,), (1,)))
    scor = dot(codes, codes, ((1,), (1,)))
    gate = (-(LOSS_SCALE * WEIGHT_SELF) * (tcorr - SHIFT_SELF) * jnp.maximum(scor, 0.0)).astype(jnp.bfloat16)
    self_ref[...] = dot(gate, codes) + dot(gate, codes, ((0,), (0,)))

    for o in range(3):
        part = held[o].at[pl.ds(0, RING * (SIDE - 1))]
        remote(part, part, send2.at[o], recv2.at[o], me).wait()
    spans = [(pl.ds(pl.multiple_of((where[o][1] >> 2) * 16, 16), 16),
              pl.ds(pl.multiple_of(512 * o + (where[o][1] & 3) * 128, 128), 128)) for o in range(3)]

    def pick(o, step):
        layer, spot = where[o]
        asker = device_at(o, layer, shifted(spot, step))
        for k in range(KNN):
            up, at = place(o, nb_ref[k, asker])
            picked[o, step, k] = held[o][(up << 5) + at]
        return asker

    for o in range(3):
        pick(o, 0)
        pltpu.make_async_copy(picked.at[o, 0], partner_ref.at[:, spans[o][0], spans[o][1]], own_sem.at[o]).start()

    def serve(step, carry):
        for o in range(3):
            asker = pick(o, step)
            remote(
                picked.at[o, step], partner_ref.at[:, spans[o][0], spans[o][1]], send3.at[o], recv3.at[o], asker
            ).start()
        return carry

    lax.fori_loop(1, RING, serve, 0)

    row = lax.broadcasted_iota(jnp.int32, (1024, 768), 0)
    col = lax.broadcasted_iota(jnp.int32, (1024, 768), 1)
    perm_ref[...] = jnp.where(col == ((row & 7) << 7) + (row >> 3), 1.0, 0.0).astype(jnp.bfloat16)
    image = lax.broadcasted_iota(jnp.int32, (128, 128), 0)
    member = jnp.concatenate(
        [jnp.where(image == nbv_ref[k : k + 1, :], 1.0, 0.0).astype(jnp.bfloat16) for k in range(KNN)], axis=1
    )
    member_ref[...] = dot(member, perm_ref[...], ((1,), (1,))).astype(jnp.bfloat16)
    tall_ref[...] = jnp.transpose(unit_ref[...].astype(jnp.float32))
    tallp_ref[...] = jnp.zeros_like(tallp_ref)

    def spread(pair, carry):
        both = tall_ref[pl.ds(pl.multiple_of(pair * 24, 8), 24), :]
        tallp_ref[2 * pair, 0:12, :] = both[0:12]
        tallp_ref[2 * pair + 1, 0:12, :] = both[12:24]
        return carry

    lax.fori_loop(0, 64, spread, 0)

    for o in range(3):
        pltpu.make_async_copy(picked.at[o, 0], picked.at[o, 0], own_sem.at[o]).wait()
        part = picked.at[o, pl.ds(1, RING - 1)]
        remote(part, part, send3.at[o], recv3.at[o], me).wait()

    partners = partner_ref[...].reshape(KNN * 128, 1536)
    partner_code, partner_inv = code_rows(dot(partners, weight_ref[...]))
    tcorr = dot(partners, unit_ref[...], ((1,), (1,)))
    scor = dot(partner_code, code_ref[...], ((1,), (1,)))
    gate = (-(LOSS_SCALE * WEIGHT_PAIR) * (tcorr - SHIFT_PAIR) * jnp.maximum(scor, 0.0)).astype(jnp.bfloat16)
    cross = back_norm(dot(gate, code_ref[...]), partner_code, partner_inv).astype(jnp.bfloat16)
    cross_out[...] = dot(perm_ref[...], cross).reshape(128, 8, 384).astype(jnp.bfloat16)

    def give(step, carry):
        target = (((column + (step >> 3)) & 3) | ((((column >> 2) + (step >> 5)) & 3) << 2)) << 3
        target = target + (((lane >> 1) + (step >> 1)) & 3) * 2 + ((lane + step) & 1)
        remote(cross_out.at[target], cross_in.at[me], send4.at[0], recv4.at[0], target).start()
        return carry

    lax.fori_loop(1, 128, give, 0)
    cross_in[me] = cross_out[me]
    grad = self_ref[...] + dot(gate, partner_code, ((0,), (0,)))
    self_ref[...] = back_norm(grad, code_ref[...], inv_ref[:, 0:1])
    part = cross_in.at[pl.ds(0, 127)]
    remote(part, part, send4.at[0], recv4.at[0], me).wait()

    piece = dot(member_ref[...], cross_in[...].reshape(1024, 384))
    back_out[:, :, 0, :] = piece.reshape(16, 8, 384)
    for hop in range(1, 8):
        to = (((lane >> 1) + (hop >> 1)) & 3) * 2 + ((lane + hop) & 1)
        remote(back_out.at[:, to], back_mid.at[:, lane], send4.at[1], recv4.at[1], (column << 3) + to).start()
    back_mid[:, lane] = back_out[:, lane]
    part = back_out.at[:, pl.ds(0, 7)]
    remote(part, part, send4.at[1], recv4.at[1], me).wait()
    for hop in range(1, 16):
        to = (((column >> 2) + (hop >> 2)) & 3) * 4 + ((column + hop) & 3)
        remote(back_mid.at[to], back_in.at[column], send4.at[2], recv4.at[2], (to << 3) + lane).start()
    back_in[column] = back_mid[column]
    part = back_in.at[pl.ds(0, 15)]
    remote(part, part, send4.at[2], recv4.at[2], me).wait()
    relayed = back_in[:, :, 0, :].reshape(128, 384).astype(jnp.bfloat16)
    code_grad = self_ref[...] + relayed.astype(jnp.float32)
    grad_ref[0] = code_grad

    tall = tallp_ref[...].astype(jnp.bfloat16).reshape(2048, 128)
    shares = dot(tall, code_grad.astype(jnp.bfloat16)).reshape(64, 2, 16, 384).astype(jnp.bfloat16)
    share_out[0] = shares[:, 0, 0:12]
    share_out[1] = shares[:, 1, 0:12]
    sibling = remote(share_out.at[1 - core], share_mid, send4.at[3], recv4.at[3], me + 1 - 2 * core)
    sibling.start()
    sibling.wait()
    share_sum[...] = (share_out[core].astype(jnp.float32) + share_mid[...].astype(jnp.float32)).astype(jnp.bfloat16)

    def spend(step, carry):
        to = (((chip >> 4) + (step >> 4)) & 3) * 16 + (((chip >> 2) + (step >> 2)) & 3) * 4 + ((chip + step) & 3)
        remote(share_sum.at[to], share_in.at[chip], send4.at[4], recv4.at[4], to * 2 + core).start()
        return carry

    lax.fori_loop(1, 64, spend, 0)
    share_in[chip] = share_sum[chip]
    part = share_in.at[pl.ds(0, 63)]
    remote(part, part, send4.at[4], recv4.at[4], me).wait()
    head_ref[...] = jnp.sum(share_in[...].astype(jnp.float32), axis=0)


def body(teacher, head_weight, neighbours):
    smem = pl.BlockSpec(memory_space=pltpu.SMEM)
    vmem = pl.BlockSpec(memory_space=pltpu.VMEM)
    hbm = pl.BlockSpec(memory_space=pl.ANY)
    slots = jnp.transpose(neighbours)
    half, full = jnp.bfloat16, jnp.float32
    return pl.pallas_call(
        step_kernel,
        out_shape=(jax.ShapeDtypeStruct((12, 384), full), jax.ShapeDtypeStruct((1, 128, 384), full)),
        in_specs=[smem, vmem, hbm, hbm],
        out_specs=(vmem, vmem),
        scratch_shapes=[
            pltpu.VMEM((128, 1536), half),
            pltpu.VMEM((1536, 384), half),
            pltpu.VMEM((128, 1536), half),
            pltpu.VMEM((128, 384), half),
            pltpu.VMEM((128, 128), full),
            pltpu.VMEM((128, 384), full),
            pltpu.VMEM((1536, 128), full),
            pltpu.VMEM((128, 16, 128), full),
            pltpu.VMEM((1024, 768), half),
            pltpu.VMEM((128, 1024), half),
        ]
        + [pltpu.VMEM((128, 16, 128), half)] * 3
        + [
            pltpu.VMEM((3, RING, KNN, 16, 128), half),
            pltpu.VMEM((KNN, 128, 1536), half),
            pltpu.VMEM((128, 8, 384), half),
            pltpu.VMEM((128, 8, 384), half),
            pltpu.VMEM((16, 8, 1, 384), full),
            pltpu.VMEM((16, 8, 1, 384), full),
            pltpu.VMEM((16, 8, 1, 384), full),
            pltpu.VMEM((2, 64, 12, 384), half),
            pltpu.VMEM((64, 12, 384), half),
            pltpu.VMEM((64, 12, 384), half),
            pltpu.VMEM((64, 12, 384), half),
            pltpu.SemaphoreType.DMA((2,)),
        ]
        + [pltpu.SemaphoreType.DMA((3,))] * 7
        + [pltpu.SemaphoreType.DMA((5,))] * 2,
        compiler_params=pltpu.CompilerParams(
            collective_id=0, has_side_effects=True, vmem_limit_bytes=48 * 2**20
        ),
    )(slots, slots, teacher, head_weight)


def solution(mesh):
    return jax.shard_map(
        body,
        mesh=mesh,
        in_specs=(P("dp", None, None), P(), P()),
        out_specs=(P("dp", None), P("dp", None, None)),
        check_vma=False,
    )
```

```python
import jax
import jax.numpy as jnp
from jax import lax
from jax.experimental import pallas as pl
from jax.experimental.pallas import tpu as pltpu
from jax.sharding import PartitionSpec as P

EPS = 1e-06
LOSS_SCALE = 128.0
SHIFT_SELF = 0.18
WEIGHT_SELF = 0.1
SHIFT_PAIR = 0.12
WEIGHT_PAIR = 0.5
MESH = pl.DeviceIdType.MESH
SIDE = 4
RING = 32
KNN = 6


def place(orient, index):
    y, x, z, c = index >> 5, (index >> 3) & 3, (index >> 1) & 3, index & 1
    if orient == 0:
        return y, index & 31
    if orient == 1:
        return x, (y << 3) + (index & 7)
    return z, ((index >> 3) << 1) + c


def device_at(orient, layer, spot):
    if orient == 0:
        return (layer << 5) + spot
    if orient == 1:
        return ((spot >> 3) << 5) + (layer << 3) + (spot & 7)
    return ((spot >> 1) << 3) + (layer << 1) + (spot & 1)


def shifted(spot, step):
    a = ((spot >> 3) + (step >> 3)) & 3
    b = ((spot >> 1) + (step >> 1)) & 3
    return (a << 3) + (b << 1) + ((spot + step) & 1)


def remote(src, dst, send, recv, device):
    return pltpu.make_async_remote_copy(
        src_ref=src, dst_ref=dst, send_sem=send, recv_sem=recv, device_id=(device,), device_id_type=MESH
    )


def unit_rows(values):
    total = jnp.sum(values * values, axis=-1, keepdims=True)
    return (values * lax.rsqrt(total + EPS)).astype(jnp.bfloat16)


def code_rows(codes):
    values = codes.astype(jnp.bfloat16).astype(jnp.float32)
    inverse = lax.rsqrt(jnp.sum(values * values, axis=-1, keepdims=True) + EPS)
    return (values * inverse).astype(jnp.bfloat16), inverse


def back_norm(grad, code_unit, inverse):
    values = code_unit.astype(jnp.float32)
    return (grad - values * jnp.sum(values * grad, axis=-1, keepdims=True)) * inverse


def dot(a, b, dims=((1,), (0,))):
    return lax.dot_general(a, b, (dims, ((), ())), preferred_element_type=jnp.float32)


def digit_sum(place_sum, step):
    return ((((place_sum >> 2) + (step >> 2)) & 3) << 2) + ((place_sum + step) & 3)


SPLIT = ((1, 16), (4, 4), (16, 1))
GREETED = [(0, step) for step in range(1, 32)] + [(1, step) for step in range(8, 32)]
GREETED += [(2, step) for step in range(8, 32) if (step >> 1) & 3]
GREETED.sort(key=lambda at: -(min(at[1] >> 3, 4 - (at[1] >> 3)) + min((at[1] >> 1) & 3, 4 - ((at[1] >> 1) & 3))))


def step_kernel(
    nb_hbm, teacher_hbm, weight_hbm, head_ref, grad_hbm,
    nb_ref, nbv_ref, teacher_ref, weight_ref, unit_ref, both_ref, code_ref, tcode_ref, inv_ref, self_ref, grad_ref,
    perm_ref, pad_ref, member_ref, held0, held1, held2, picked, wide_ref, product_ref, share_ref,
    cross_out, cross_in, part_out, part_in, back_out, back_in,
    out0, out1, out2, mid0, mid1, mid2, sum0, sum1, sum2, in0, in1, in2, plane_out, plane_in,
    load_sem, own_sem, *sems,
):
    held, share_out, share_mid = (held0, held1, held2), (out0, out1, out2), (mid0, mid1, mid2)
    share_sum, layer_in = (sum0, sum1, sum2), (in0, in1, in2)
    pairs = [(sems[2 * i], sems[2 * i + 1]) for i in range(len(sems) // 2)]
    deal_sem, layer_sem, serve_sem, cross_sem, part_sem, back_sem, core_sem, axis_sem, plane_sem = pairs
    me = lax.axis_index("dp")
    where = [place(o, me) for o in range(3)]
    core = me & 1
    barrier = pltpu.get_barrier_semaphore()
    loads = [
        pltpu.make_async_copy(teacher_hbm.at[0], teacher_ref, load_sem.at[0]),
        pltpu.make_async_copy(weight_hbm, weight_ref, load_sem.at[1]),
        pltpu.make_async_copy(nb_hbm, nb_ref, load_sem.at[2]),
        pltpu.make_async_copy(nb_hbm, nbv_ref, load_sem.at[3]),
    ]
    for load in loads:
        load.start()

    for o, step in GREETED:
        layer, spot = where[o]
        pl.semaphore_signal(barrier, inc=1, device_id=(device_at(o, layer, shifted(spot, step)),), device_id_type=MESH)
    loads[0].wait()
    values = unit_rows(teacher_ref[...].astype(jnp.float32))
    unit_ref[...] = values
    wide_ref[:, 768:896] = jnp.transpose(values.astype(jnp.float32)).astype(jnp.bfloat16)
    for load in loads[1:]:
        load.wait()
    pl.semaphore_wait(barrier, len(GREETED))

    def tile(o, spot):
        return wide_ref.at[pl.ds(pl.multiple_of(512 * o + spot * 16, 16), 16), pl.ds(768, 128)]

    own = []
    for o in range(3):
        layer, spot = where[o]

        def deal(step, carry):
            target = shifted(spot, step)
            remote(
                tile(o, target), held[o].at[layer * RING + spot], deal_sem[0].at[o], deal_sem[1].at[o],
                device_at(o, layer, target),
            ).start()
            return carry

        lax.fori_loop(1, RING, deal, 0)
        own.append(pltpu.make_async_copy(tile(o, spot), held[o].at[layer * RING + spot], own_sem.at[o]))
        own[o].start()

    code_unit, inverse = code_rows(dot(unit_ref[...], weight_ref[...]))
    code_ref[...] = code_unit
    inv_ref[...] = jnp.broadcast_to(inverse, inv_ref.shape)

    for o in range(3):
        layer, spot = where[o]
        own[o].wait()
        part = held[o].at[pl.ds(0, RING - 1)]
        remote(part, part, deal_sem[0].at[o], deal_sem[1].at[o], me).wait()
        mine = held[o].at[pl.ds(layer * RING, RING)]
        for hop in range(1, SIDE):
            remote(mine, mine, layer_sem[0].at[o], layer_sem[1].at[o], device_at(o, (layer + hop) & 3, spot)).start()

    units, codes = unit_ref[...], code_ref[...]
    tcorr = dot(units, units, ((1,), (1,)))
    scor = dot(codes, codes, ((1,), (1,)))
    gate = (-(LOSS_SCALE * WEIGHT_SELF) * (tcorr - SHIFT_SELF) * jnp.maximum(scor, 0.0)).astype(jnp.bfloat16)
    self_ref[...] = dot(gate, codes) + dot(gate, codes, ((0,), (0,)))

    for o in range(3):
        layer, spot = where[o]
        part = held[o].at[pl.ds(0, RING * (SIDE - 1))]
        remote(part, part, layer_sem[0].at[o], layer_sem[1].at[o], me).wait()
        rows, cols = pl.ds(pl.multiple_of(512 * o + spot * 16, 16), 16), pl.ds(0, 768)

        def pick(step):
            asker = device_at(o, layer, shifted(spot, step))
            for k in range(KNN):
                up, at = place(o, nb_ref[k, asker])
                picked[o, step, :, 128 * k : 128 * (k + 1)] = held[o][(up << 5) + at]
            return asker

        def serve(step, carry):
            asker = pick(step)
            remote(
                picked.at[o, step], wide_ref.at[rows, cols], serve_sem[0].at[o], serve_sem[1].at[o], asker
            ).start()
            return carry

        lax.fori_loop(1, RING, serve, 0)
        pick(0)
        pltpu.make_async_copy(picked.at[o, 0], wide_ref.at[rows, cols], own_sem.at[o]).start()

    both_ref[0:384, :] = jnp.transpose(weight_ref[...].astype(jnp.float32)).astype(jnp.bfloat16)
    both_ref[384:512, :] = unit_ref[...]
    tcode_ref[...] = jnp.transpose(code_ref[...].astype(jnp.float32)).astype(jnp.bfloat16)
    row = lax.broadcasted_iota(jnp.int32, (768, 768), 0)
    col = lax.broadcasted_iota(jnp.int32, (768, 768), 1)
    perm_ref[...] = jnp.where(
        (row % 24 == ((col >> 7) << 2) + (col & 3)) & (row // 24 == ((col >> 2) & 31)), 1.0, 0.0
    ).astype(jnp.bfloat16)
    row = lax.broadcasted_iota(jnp.int32, (256, 128), 0)
    col = lax.broadcasted_iota(jnp.int32, (256, 128), 1)
    pad_ref[...] = jnp.where(((row >> 3) == (col >> 2)) & ((row & 7) == (col & 3)), 1.0, 0.0).astype(jnp.bfloat16)
    slots = nbv_ref[...].astype(jnp.float32).astype(jnp.bfloat16)
    slot_of = (lax.broadcasted_iota(jnp.int32, (KNN, 768), 1) % 24) >> 2
    mine = slot_of == lax.broadcasted_iota(jnp.int32, (KNN, 768), 0)
    image = lax.broadcasted_iota(jnp.int32, (128, 768), 0)
    source = lax.broadcasted_iota(jnp.int32, (128, 768), 1) // 24
    row = lax.broadcasted_iota(jnp.int32, (512, 768), 0)
    same = (row & 3) == (lax.broadcasted_iota(jnp.int32, (512, 768), 1) & 3)
    for o in range(3):
        layer, spot = where[o]
        chosen = jnp.where(image == device_at(o, layer, source), 1.0, 0.0).astype(jnp.bfloat16)
        named = jnp.sum(jnp.where(mine, dot(slots, chosen), 0.0), axis=0, keepdims=True)
        owner = device_at(o, row >> 7, (row >> 2) & 31).astype(jnp.float32)
        member_ref[o] = jnp.where(same & (owner == named), 1.0, 0.0).astype(jnp.bfloat16)

    for o in range(3):
        pltpu.make_async_copy(picked.at[o, 0], picked.at[o, 0], own_sem.at[o]).wait()
        part = picked.at[o, pl.ds(1, RING - 1)]
        remote(part, part, serve_sem[0].at[o], serve_sem[1].at[o], me).wait()
        third = slice(512 * o, 512 * (o + 1))
        product = dot(both_ref[:, third], wide_ref[third, 0:768])
        product_ref[...] = product if o == 0 else product_ref[...] + product

    values = product_ref[0:384, :].astype(jnp.bfloat16).astype(jnp.float32)
    partner_inv = lax.rsqrt(jnp.sum(values * values, axis=0, keepdims=True) + EPS)
    partner_code = (values * partner_inv).astype(jnp.bfloat16)
    tcorr = product_ref[384:512, :]
    scor = dot(code_ref[...], partner_code)
    gate = (-(LOSS_SCALE * WEIGHT_PAIR) * (tcorr - SHIFT_PAIR) * jnp.maximum(scor, 0.0)).astype(jnp.bfloat16)
    raw = dot(tcode_ref[...], gate)
    values = partner_code.astype(jnp.float32)
    cross = ((raw - values * jnp.sum(values * raw, axis=0, keepdims=True)) * partner_inv).astype(jnp.bfloat16)
    cross_out[...] = dot(perm_ref[...], cross, ((1,), (1,))).reshape(RING, 24, 384).astype(jnp.bfloat16)

    for o in range(3):
        layer, spot = where[o]

        def give(step, carry):
            target = shifted(spot, step)
            remote(
                cross_out.at[target, :, pl.ds(128 * o, 128)], cross_in.at[o, spot], cross_sem[0].at[o], cross_sem[1].at[o],
                device_at(o, layer, target),
            ).start()
            return carry

        lax.fori_loop(1, RING, give, 0)
        cross_in[o, spot] = cross_out[spot, :, 128 * o : 128 * (o + 1)]

    grad = self_ref[...] + dot(gate, partner_code, ((1,), (1,)))
    own_grad = back_norm(grad, code_ref[...], inv_ref[:, 0:1])
    self_ref[...] = own_grad

    coarse = own_grad.astype(jnp.bfloat16)
    fine = (own_grad - coarse.astype(jnp.float32)).astype(jnp.bfloat16)
    share_ref[0:1536, :] = (
        dot(wide_ref[:, 0:768], cross, ((1,), (1,))) + dot(wide_ref[:, 768:896], coarse) + dot(wide_ref[:, 768:896], fine)
    )

    def cut(chip, carry):
        first = share_ref[pl.ds(pl.multiple_of(chip * 24, 8), 16), :].astype(jnp.bfloat16)
        second = share_ref[pl.ds(pl.multiple_of(chip * 24 + 8, 8), 24), :][4:20].astype(jnp.bfloat16)
        for o, at in enumerate(((0, chip >> 4, chip & 15), (chip >> 4, (chip >> 2) & 3, chip & 3), (chip >> 2, chip & 3, 0))):
            share_out[o][0, at[0], at[1], at[2]] = first[:, 128 * o : 128 * (o + 1)]
            share_out[o][1, at[0], at[1], at[2]] = second[:, 128 * o : 128 * (o + 1)]
        return carry

    lax.fori_loop(0, 64, cut, 0)
    for o in range(3):
        remote(share_out[o].at[1 - core], share_mid[o], core_sem[0].at[o], core_sem[1].at[o], me + 1 - 2 * core).start()

    for o in range(3):
        layer, spot = where[o]
        part = cross_in.at[o, pl.ds(0, RING - 1)]
        remote(part, part, cross_sem[0].at[o], cross_sem[1].at[o], me).wait()
        piece = dot(member_ref[o], cross_in[o].reshape(768, 128))
        part_out[o] = piece.astype(jnp.bfloat16).reshape(4, 128, 128)
        for hop in range(1, SIDE):
            to = (layer + hop) & 3
            remote(
                part_out.at[o, to], part_in.at[o, layer], part_sem[0].at[o], part_sem[1].at[o], device_at(o, to, spot)
            ).start()
        part_in[o, layer] = part_out[o, layer]

    for o in range(3):
        layer, spot = where[o]
        remote(share_out[o].at[0], share_mid[o], core_sem[0].at[o], core_sem[1].at[o], me).wait()
        total = share_out[o][core].astype(jnp.float32) + share_mid[o][...].astype(jnp.float32)
        share_sum[o][...] = total.astype(jnp.bfloat16)
        for hop in range(1, SIDE):
            to = (layer + hop) & 3
            remote(
                share_sum[o].at[:, to], layer_in[o].at[layer], axis_sem[0].at[o], axis_sem[1].at[o], device_at(o, to, spot)
            ).start()
        layer_in[o][layer] = share_sum[o][:, layer]
    for o in range(3):
        layer, spot = where[o]
        part = part_in.at[o, pl.ds(0, SIDE - 1)]
        remote(part, part, part_sem[0].at[o], part_sem[1].at[o], me).wait()
        relayed = jnp.sum(part_in[o].astype(jnp.float32), axis=0).astype(jnp.bfloat16)
        back_out[o] = dot(pad_ref[...], relayed).reshape(RING, 8, 128).astype(jnp.bfloat16)

        def give_back(step, carry):
            target = shifted(spot, step)
            remote(
                back_out.at[o, target], back_in.at[o, spot], back_sem[0].at[o], back_sem[1].at[o],
                device_at(o, layer, target),
            ).start()
            return carry

        lax.fori_loop(1, RING, give_back, 0)
        back_in[o, spot] = back_out[o, spot]

    for o in range(3):
        layer, spot = where[o]
        at = spot >> 1
        part = layer_in[o].at[pl.ds(0, SIDE - 1)]
        remote(part, part, axis_sem[0].at[o], axis_sem[1].at[o], me).wait()
        total = jnp.sum(layer_in[o][...].astype(jnp.float32), axis=0)
        plane_out[o] = total.astype(jnp.bfloat16).reshape(16, 16, 128)
        for step in range(1, 16):
            to = digit_sum(at, step)
            remote(
                plane_out.at[o, to], plane_in.at[o, at], plane_sem[0].at[o], plane_sem[1].at[o],
                device_at(o, layer, (to << 1) + core),
            ).start()
        plane_in[o, at] = plane_out[o, at]
    for o in range(3):
        lanes = slice(128 * o, 128 * (o + 1))
        part = back_in.at[o, pl.ds(0, RING - 1)]
        remote(part, part, back_sem[0].at[o], back_sem[1].at[o], me).wait()
        relayed = dot(pad_ref[...], back_in[o].reshape(256, 128), ((0,), (0,)))
        grad_ref[:, lanes] = self_ref[:, lanes] + relayed
    grad_copy = pltpu.make_async_copy(grad_ref, grad_hbm.at[0], load_sem.at[0])
    grad_copy.start()
    for o in range(3):
        part = plane_in.at[o, pl.ds(0, 15)]
        remote(part, part, plane_sem[0].at[o], plane_sem[1].at[o], me).wait()
        total = jnp.sum(plane_in[o].astype(jnp.float32), axis=0)
        head_ref[:, 128 * o : 128 * (o + 1)] = total[0:12]
    grad_copy.wait()


def body(teacher, head_weight, neighbours):
    vmem = pl.BlockSpec(memory_space=pltpu.VMEM)
    hbm = pl.BlockSpec(memory_space=pl.ANY)
    half, full = jnp.bfloat16, jnp.float32
    return pl.pallas_call(
        step_kernel,
        out_shape=(jax.ShapeDtypeStruct((12, 384), full), jax.ShapeDtypeStruct((1, 128, 384), full)),
        in_specs=[hbm, hbm, hbm],
        out_specs=(vmem, hbm),
        scratch_shapes=[
            pltpu.SMEM((KNN, 128), jnp.int32),
            pltpu.VMEM((KNN, 128), jnp.int32),
            pltpu.VMEM((128, 1536), half),
            pltpu.VMEM((1536, 384), half),
            pltpu.VMEM((128, 1536), half),
            pltpu.VMEM((512, 1536), half),
            pltpu.VMEM((128, 384), half),
            pltpu.VMEM((384, 128), half),
            pltpu.VMEM((128, 128), full),
            pltpu.VMEM((128, 384), full),
            pltpu.VMEM((128, 384), full),
            pltpu.VMEM((768, 768), half),
            pltpu.VMEM((256, 128), half),
            pltpu.VMEM((3, 512, 768), half),
        ]
        + [pltpu.VMEM((128, 16, 128), half)] * 3
        + [
            pltpu.VMEM((3, RING, 16, KNN * 128), half),
            pltpu.VMEM((1536, 896), half),
            pltpu.VMEM((512, 768), full),
            pltpu.VMEM((1544, 384), full),
            pltpu.VMEM((RING, 24, 384), half),
            pltpu.VMEM((3, RING, 24, 128), half),
            pltpu.VMEM((3, 4, 128, 128), half),
            pltpu.VMEM((3, 4, 128, 128), half),
            pltpu.VMEM((3, RING, 8, 128), half),
            pltpu.VMEM((3, RING, 8, 128), half),
        ]
        + [pltpu.VMEM((2, a, 4, b, 16, 128), half) for a, b in SPLIT]
        + [pltpu.VMEM((a, 4, b, 16, 128), half) for a, b in SPLIT] * 2
        + [pltpu.VMEM((4, a, b, 16, 128), half) for a, b in SPLIT]
        + [pltpu.VMEM((3, 16, 16, 128), half)] * 2
        + [pltpu.SemaphoreType.DMA((4,)), pltpu.SemaphoreType.DMA((3,))]
        + [pltpu.SemaphoreType.DMA((3,))] * 18,
        compiler_params=pltpu.CompilerParams(
            collective_id=0, has_side_effects=True, vmem_limit_bytes=63 * 2**20
        ),
    )(jnp.transpose(neighbours), teacher, head_weight)


def solution(mesh):
    return jax.shard_map(
        body,
        mesh=mesh,
        in_specs=(P("dp", None, None), P(), P()),
        out_specs=(P("dp", None), P("dp", None, None)),
        check_vma=False,
    )
```

```python
import jax
import jax.numpy as jnp
from jax import lax
from jax.experimental import pallas as pl
from jax.experimental.pallas import tpu as pltpu
from jax.sharding import PartitionSpec as P

EPS = 1e-06
LOSS_SCALE = 128.0
SHIFT_SELF = 0.18
WEIGHT_SELF = 0.1
SHIFT_PAIR = 0.12
WEIGHT_PAIR = 0.5
MESH = pl.DeviceIdType.MESH
SIDE = 4
RING = 32
KNN = 6


def place(orient, index):
    y, x, z, c = index >> 5, (index >> 3) & 3, (index >> 1) & 3, index & 1
    if orient == 0:
        return y, index & 31
    if orient == 1:
        return x, (y << 3) + (index & 7)
    return z, ((index >> 3) << 1) + c


def device_at(orient, layer, spot):
    if orient == 0:
        return (layer << 5) + spot
    if orient == 1:
        return ((spot >> 3) << 5) + (layer << 3) + (spot & 7)
    return ((spot >> 1) << 3) + (layer << 1) + (spot & 1)


def shifted(spot, step):
    a = ((spot >> 3) + (step >> 3)) & 3
    b = ((spot >> 1) + (step >> 1)) & 3
    return (a << 3) + (b << 1) + ((spot + step) & 1)


def remote(src, dst, send, recv, device):
    return pltpu.make_async_remote_copy(
        src_ref=src, dst_ref=dst, send_sem=send, recv_sem=recv, device_id=(device,), device_id_type=MESH
    )


def unit_rows(values):
    total = jnp.sum(values * values, axis=-1, keepdims=True)
    return (values * lax.rsqrt(total + EPS)).astype(jnp.bfloat16)


def code_rows(codes):
    values = codes.astype(jnp.bfloat16).astype(jnp.float32)
    inverse = lax.rsqrt(jnp.sum(values * values, axis=-1, keepdims=True) + EPS)
    return (values * inverse).astype(jnp.bfloat16), inverse


def back_norm(grad, code_unit, inverse):
    values = code_unit.astype(jnp.float32)
    return (grad - values * jnp.sum(values * grad, axis=-1, keepdims=True)) * inverse


def dot(a, b, dims=((1,), (0,))):
    return lax.dot_general(a, b, (dims, ((), ())), preferred_element_type=jnp.float32)


def digit_sum(place_sum, step):
    return ((((place_sum >> 2) + (step >> 2)) & 3) << 2) + ((place_sum + step) & 3)


SPLIT = ((1, 16), (4, 4), (16, 1))
GREETED = [(0, step) for step in range(1, 32)] + [(1, step) for step in range(8, 32)]
GREETED += [(2, step) for step in range(8, 32) if (step >> 1) & 3]
GREETED.sort(key=lambda at: -(min(at[1] >> 3, 4 - (at[1] >> 3)) + min((at[1] >> 1) & 3, 4 - ((at[1] >> 1) & 3))))


def step_kernel(
    nb_hbm, teacher_hbm, weight_hbm, head_ref, grad_ref,
    table_ref, tablev_ref, nbv_ref, teacher_ref, weight_ref, unit_ref, both_ref, code_ref, tcode_ref, inv_ref, self_ref,
    perm_ref, swap_ref, member_ref, stage, held0, held1, held2, picked, wide_ref, product_ref, share_ref,
    cross_out, cross_in, part_out, part_in,
    out0, out1, out2, mid0, mid1, mid2, sum0, sum1, sum2, in0, in1, in2, tail_out, tail_in,
    load_sem, own_sem, *sems,
):
    held, share_out, share_mid = (held0, held1, held2), (out0, out1, out2), (mid0, mid1, mid2)
    share_sum, layer_in = (sum0, sum1, sum2), (in0, in1, in2)
    pairs = [(sems[2 * i], sems[2 * i + 1]) for i in range(len(sems) // 2)]
    deal_sem, layer_sem, serve_sem, cross_sem, part_sem, core_sem, axis_sem, tail_sem = pairs
    me = lax.axis_index("dp")
    where = [place(o, me) for o in range(3)]
    core = me & 1
    barrier = pltpu.get_barrier_semaphore()
    loads = [
        pltpu.make_async_copy(teacher_hbm.at[0], teacher_ref, load_sem.at[0]),
        pltpu.make_async_copy(weight_hbm, weight_ref, load_sem.at[1]),
        pltpu.make_async_copy(nb_hbm, nbv_ref, load_sem.at[2]),
    ]
    for load in loads:
        load.start()

    for o, step in GREETED:
        layer, spot = where[o]
        pl.semaphore_signal(barrier, inc=1, device_id=(device_at(o, layer, shifted(spot, step)),), device_id_type=MESH)
    loads[0].wait()
    values = unit_rows(teacher_ref[...].astype(jnp.float32))
    unit_ref[...] = values
    wide_ref[:, 768:896] = jnp.transpose(values.astype(jnp.float32)).astype(jnp.bfloat16)
    for load in loads[1:]:
        load.wait()
    named = nbv_ref[...]
    for o in range(3):
        up, at = place(o, named)
        tablev_ref[o, 0:KNN, :] = (up << 5) + ((at & 1) << 4) + (at >> 1)
        tablev_ref[o, KNN:8, :] = jnp.zeros((2, 128), jnp.int32)
    table_load = pltpu.make_async_copy(tablev_ref, table_ref, load_sem.at[3])
    table_load.start()
    table_load.wait()
    pl.semaphore_wait(barrier, len(GREETED))

    def tile(o, at):
        return wide_ref.at[pl.ds(pl.multiple_of(512 * o + at * 32, 32), 32), pl.ds(768, 128)]

    own = []
    for o in range(3):
        layer, spot = where[o]
        at = spot >> 1

        def deal(step, carry):
            to = digit_sum(at, step)
            remote(
                tile(o, to), stage.at[o, at], deal_sem[0].at[o], deal_sem[1].at[o],
                device_at(o, layer, (to << 1) + core),
            ).start()
            return carry

        lax.fori_loop(1, 16, deal, 0)
        own.append(pltpu.make_async_copy(tile(o, at), stage.at[o, at], own_sem.at[o]))
        own[o].start()

    code_unit, inverse = code_rows(dot(unit_ref[...], weight_ref[...]))
    code_ref[...] = code_unit
    inv_ref[...] = jnp.broadcast_to(inverse, inv_ref.shape)

    for o in range(3):
        layer, spot = where[o]
        own[o].wait()
        part = stage.at[o, pl.ds(0, 15)]
        remote(part, part, deal_sem[0].at[o], deal_sem[1].at[o], me).wait()
        mine = held[o].at[pl.ds((layer * 2 + core) * 16, 16)]
        for hop in range(1, 8):
            up, side = (layer + (hop >> 1)) & 3, (core + hop) & 1
            remote(
                stage.at[o, :, pl.ds(pl.multiple_of(side * 16, 16), 16)], mine, layer_sem[0].at[o], layer_sem[1].at[o],
                device_at(o, up, spot - core + side),
            ).start()
        own[o] = pltpu.make_async_copy(stage.at[o, :, pl.ds(pl.multiple_of(core * 16, 16), 16)], mine, own_sem.at[o])
        own[o].start()

    units, codes = unit_ref[...], code_ref[...]
    tcorr = dot(units, units, ((1,), (1,)))
    scor = dot(codes, codes, ((1,), (1,)))
    gate = (-(LOSS_SCALE * WEIGHT_SELF) * (tcorr - SHIFT_SELF) * jnp.maximum(scor, 0.0)).astype(jnp.bfloat16)
    self_ref[...] = dot(gate, codes) + dot(gate, codes, ((0,), (0,)))

    both_ref[0:384, :] = jnp.transpose(weight_ref[...].astype(jnp.float32)).astype(jnp.bfloat16)
    both_ref[384:512, :] = units
    tcode_ref[...] = jnp.transpose(codes.astype(jnp.float32)).astype(jnp.bfloat16)
    row = lax.broadcasted_iota(jnp.int32, (768, 128), 0)
    col = lax.broadcasted_iota(jnp.int32, (768, 128), 1)
    block = (row * 2731) >> 16
    within = jnp.where(block == (col >> 2), row - 24 * block - (col & 3), -1)
    for k in range(KNN):
        perm_ref[:, 128 * k : 128 * (k + 1)] = jnp.where(within == 4 * k, 1.0, 0.0).astype(jnp.bfloat16)
    row = lax.broadcasted_iota(jnp.int32, (128, 128), 0)
    col = lax.broadcasted_iota(jnp.int32, (128, 128), 1)
    swap_ref[...] = jnp.where(
        col == (((row >> 2) & 1) << 6) + ((row >> 3) << 2) + (row & 3), 1.0, 0.0
    ).astype(jnp.bfloat16)

    spans = []
    for o in range(3):
        layer, spot = where[o]
        own[o].wait()
        part = held[o].at[pl.ds(0, 7 * 16)]
        remote(part, part, layer_sem[0].at[o], layer_sem[1].at[o], me).wait()
        spans.append((pl.ds(pl.multiple_of(512 * o + spot * 16, 16), 16), pl.ds(0, 768)))

    def pick(o, step):
        layer, spot = where[o]
        asker = device_at(o, layer, shifted(spot, step))
        for k in range(KNN):
            picked[o, step, :, 128 * k : 128 * (k + 1)] = held[o][table_ref[o, k, asker]]
        return asker

    def serve(step, carry):
        for o in range(3):
            asker = pick(o, step)
            remote(
                picked.at[o, step], wide_ref.at[spans[o][0], spans[o][1]], serve_sem[0].at[o], serve_sem[1].at[o], asker
            ).start()
        return carry

    lax.fori_loop(1, RING, serve, 0)
    for o in range(3):
        pick(o, 0)
        pltpu.make_async_copy(picked.at[o, 0], wide_ref.at[spans[o][0], spans[o][1]], own_sem.at[o]).start()

    slots = nbv_ref[...].astype(jnp.float32).astype(jnp.bfloat16)
    col = lax.broadcasted_iota(jnp.int32, (1, 768), 1)
    source = (col * 2731) >> 16
    slot_of = (col - 24 * source) >> 2
    mine = lax.broadcasted_iota(jnp.int32, (KNN, 768), 0) == slot_of
    image = lax.broadcasted_iota(jnp.int32, (128, 768), 0)
    row = lax.broadcasted_iota(jnp.int32, (512, 128), 0)
    same = (row & 3) == (lax.broadcasted_iota(jnp.int32, (512, 128), 1) & 3)
    for o in range(3):
        layer, spot = where[o]
        chosen = jnp.where(image == device_at(o, layer, source), 1.0, 0.0).astype(jnp.bfloat16)
        named = jnp.sum(jnp.where(mine, dot(slots, chosen), 0.0), axis=0, keepdims=True)
        owner = device_at(o, row >> 7, (((row >> 2) & 15) << 1) + ((row >> 6) & 1))
        owner = jnp.where(same, owner, -1).astype(jnp.float32)
        for k in range(KNN):
            lanes = slice(128 * k, 128 * (k + 1))
            member_ref[o, :, lanes] = jnp.where(owner == named[:, lanes], 1.0, 0.0).astype(jnp.bfloat16)

    for o in range(3):
        pltpu.make_async_copy(picked.at[o, 0], picked.at[o, 0], own_sem.at[o]).wait()
        part = picked.at[o, pl.ds(1, RING - 1)]
        remote(part, part, serve_sem[0].at[o], serve_sem[1].at[o], me).wait()
        third = slice(512 * o, 512 * (o + 1))
        product = dot(both_ref[:, third], wide_ref[third, 0:768])
        product_ref[...] = product if o == 0 else product_ref[...] + product

    values = product_ref[0:384, :].astype(jnp.bfloat16).astype(jnp.float32)
    partner_inv = lax.rsqrt(jnp.sum(values * values, axis=0, keepdims=True) + EPS)
    partner_code = (values * partner_inv).astype(jnp.bfloat16)
    tcorr = product_ref[384:512, :]
    scor = dot(code_ref[...], partner_code)
    gate = (-(LOSS_SCALE * WEIGHT_PAIR) * (tcorr - SHIFT_PAIR) * jnp.maximum(scor, 0.0)).astype(jnp.bfloat16)
    raw = dot(tcode_ref[...], gate)
    values = partner_code.astype(jnp.float32)
    cross = ((raw - values * jnp.sum(values * raw, axis=0, keepdims=True)) * partner_inv).astype(jnp.bfloat16)
    cross_out[...] = dot(perm_ref[...], cross, ((1,), (1,))).reshape(RING, 24, 384).astype(jnp.bfloat16)

    def give(step, carry):
        for o in range(3):
            layer, spot = where[o]
            target = shifted(spot, step)
            remote(
                cross_out.at[target, :, pl.ds(128 * o, 128)], cross_in.at[o, spot], cross_sem[0].at[o], cross_sem[1].at[o],
                device_at(o, layer, target),
            ).start()
        return carry

    lax.fori_loop(1, RING, give, 0)
    for o in range(3):
        spot = where[o][1]
        cross_in[o, spot] = cross_out[spot, :, 128 * o : 128 * (o + 1)]

    grad = self_ref[...] + dot(gate, partner_code, ((1,), (1,)))
    own_grad = back_norm(grad, code_ref[...], inv_ref[:, 0:1])
    self_ref[...] = own_grad

    coarse = own_grad.astype(jnp.bfloat16)
    fine = (own_grad - coarse.astype(jnp.float32)).astype(jnp.bfloat16)
    share_ref[0:1536, :] = (
        dot(wide_ref[:, 0:768], cross, ((1,), (1,))) + dot(wide_ref[:, 768:896], coarse) + dot(wide_ref[:, 768:896], fine)
    )

    def cut(chip, carry):
        first = share_ref[pl.ds(pl.multiple_of(chip * 24, 8), 16), :].astype(jnp.bfloat16)
        second = share_ref[pl.ds(pl.multiple_of(chip * 24 + 8, 8), 24), :][4:20].astype(jnp.bfloat16)
        for o, at in enumerate(((0, chip >> 4, chip & 15), (chip >> 4, (chip >> 2) & 3, chip & 3), (chip >> 2, chip & 3, 0))):
            share_out[o][0, at[0], at[1], at[2]] = first[:, 128 * o : 128 * (o + 1)]
            share_out[o][1, at[0], at[1], at[2]] = second[:, 128 * o : 128 * (o + 1)]
        return carry

    lax.fori_loop(0, 64, cut, 0)
    for o in range(3):
        remote(share_out[o].at[1 - core], share_mid[o], core_sem[0].at[o], core_sem[1].at[o], me + 1 - 2 * core).start()

    for o in range(3):
        layer, spot = where[o]
        remote(share_out[o].at[0], share_mid[o], core_sem[0].at[o], core_sem[1].at[o], me).wait()
        total = share_out[o][core].astype(jnp.float32) + share_mid[o][...].astype(jnp.float32)
        share_sum[o][...] = total.astype(jnp.bfloat16)
        for hop in range(1, SIDE):
            to = (layer + hop) & 3
            remote(
                share_sum[o].at[:, to], layer_in[o].at[layer], axis_sem[0].at[o], axis_sem[1].at[o], device_at(o, to, spot)
            ).start()
        layer_in[o][layer] = share_sum[o][:, layer]

    for o in range(3):
        layer, spot = where[o]
        part = cross_in.at[o, pl.ds(0, RING - 1)]
        remote(part, part, cross_sem[0].at[o], cross_sem[1].at[o], me).wait()
        piece = dot(member_ref[o], cross_in[o].reshape(768, 128))
        part_out[o] = piece.astype(jnp.bfloat16).reshape(8, 64, 128)
        mine = layer * 2 + core
        for hop in range(1, 8):
            up, side = (layer + (hop >> 1)) & 3, (core + hop) & 1
            remote(
                part_out.at[o, up * 2 + side], part_in.at[o, mine], part_sem[0].at[o], part_sem[1].at[o],
                device_at(o, up, spot - core + side),
            ).start()
        part_in[o, mine] = part_out[o, mine]

    for o in range(3):
        layer, spot = where[o]
        at = spot >> 1
        part = part_in.at[o, pl.ds(0, 7)]
        remote(part, part, part_sem[0].at[o], part_sem[1].at[o], me).wait()
        relayed = jnp.sum(part_in[o].reshape(4, 128, 128).astype(jnp.float32), axis=0).astype(jnp.bfloat16)
        tail_out[o, :, 16:24] = dot(swap_ref[...], relayed).reshape(16, 8, 128).astype(jnp.bfloat16)
        part = layer_in[o].at[pl.ds(0, SIDE - 1)]
        remote(part, part, axis_sem[0].at[o], axis_sem[1].at[o], me).wait()
        total = jnp.sum(layer_in[o][...].astype(jnp.float32), axis=0)
        tail_out[o, :, 0:16] = total.astype(jnp.bfloat16).reshape(16, 16, 128)

        def finish(step, carry):
            to = digit_sum(at, step)
            remote(
                tail_out.at[o, to], tail_in.at[o, at], tail_sem[0].at[o], tail_sem[1].at[o],
                device_at(o, layer, (to << 1) + core),
            ).start()
            return carry

        lax.fori_loop(1, 16, finish, 0)
        tail_in[o, at] = tail_out[o, at]

    for o in range(3):
        lanes = slice(128 * o, 128 * (o + 1))
        part = tail_in.at[o, pl.ds(0, 15)]
        remote(part, part, tail_sem[0].at[o], tail_sem[1].at[o], me).wait()
        relayed = tail_in[o, :, 16:24].astype(jnp.float32).reshape(128, 128)
        grad_ref[0, :, lanes] = self_ref[:, lanes] + relayed
        total = jnp.sum(tail_in[o, :, 0:16].astype(jnp.float32), axis=0)
        head_ref[:, lanes] = total[0:12]


def body(teacher, head_weight, neighbours):
    vmem = pl.BlockSpec(memory_space=pltpu.VMEM)
    hbm = pl.BlockSpec(memory_space=pl.ANY)
    half, full = jnp.bfloat16, jnp.float32
    return pl.pallas_call(
        step_kernel,
        out_shape=(jax.ShapeDtypeStruct((12, 384), full), jax.ShapeDtypeStruct((1, 128, 384), full)),
        in_specs=[hbm, hbm, hbm],
        out_specs=(vmem, vmem),
        scratch_shapes=[
            pltpu.SMEM((3, 8, 128), jnp.int32),
            pltpu.VMEM((3, 8, 128), jnp.int32),
            pltpu.VMEM((KNN, 128), jnp.int32),
            pltpu.VMEM((128, 1536), half),
            pltpu.VMEM((1536, 384), half),
            pltpu.VMEM((128, 1536), half),
            pltpu.VMEM((512, 1536), half),
            pltpu.VMEM((128, 384), half),
            pltpu.VMEM((384, 128), half),
            pltpu.VMEM((128, 128), full),
            pltpu.VMEM((128, 384), full),
            pltpu.VMEM((768, 768), half),
            pltpu.VMEM((128, 128), half),
            pltpu.VMEM((3, 512, 768), half),
            pltpu.VMEM((3, 16, 32, 128), half),
        ]
        + [pltpu.VMEM((128, 16, 128), half)] * 3
        + [
            pltpu.VMEM((3, RING, 16, KNN * 128), half),
            pltpu.VMEM((1536, 896), half),
            pltpu.VMEM((512, 768), full),
            pltpu.VMEM((1544, 384), full),
            pltpu.VMEM((RING, 24, 384), half),
            pltpu.VMEM((3, RING, 24, 128), half),
            pltpu.VMEM((3, 8, 64, 128), half),
            pltpu.VMEM((3, 8, 64, 128), half),
        ]
        + [pltpu.VMEM((2, a, 4, b, 16, 128), half) for a, b in SPLIT]
        + [pltpu.VMEM((a, 4, b, 16, 128), half) for a, b in SPLIT] * 2
        + [pltpu.VMEM((4, a, b, 16, 128), half) for a, b in SPLIT]
        + [pltpu.VMEM((3, 16, 24, 128), half)] * 2
        + [pltpu.SemaphoreType.DMA((4,)), pltpu.SemaphoreType.DMA((3,))]
        + [pltpu.SemaphoreType.DMA((3,))] * 16,
        compiler_params=pltpu.CompilerParams(
            collective_id=0, has_side_effects=True, vmem_limit_bytes=(65536 - 10752) * 1024
        ),
    )(jnp.transpose(neighbours), teacher, head_weight)


def solution(mesh):
    return jax.shard_map(
        body,
        mesh=mesh,
        in_specs=(P("dp", None, None), P(), P()),
        out_specs=(P("dp", None), P("dp", None, None)),
        check_vma=False,
    )
```

```python
import jax
import jax.numpy as jnp
from jax import lax
from jax.experimental import pallas as pl
from jax.experimental.pallas import tpu as pltpu
from jax.sharding import PartitionSpec as P

EPS = 1e-06
LOSS_SCALE = 128.0
SHIFT_SELF = 0.18
WEIGHT_SELF = 0.1
SHIFT_PAIR = 0.12
WEIGHT_PAIR = 0.5
MESH = pl.DeviceIdType.MESH
SIDE = 4
RING = 32
KNN = 6


def place(orient, index):
    y, x, z, c = index >> 5, (index >> 3) & 3, (index >> 1) & 3, index & 1
    if orient == 0:
        return y, index & 31
    if orient == 1:
        return x, (y << 3) + (index & 7)
    return z, ((index >> 3) << 1) + c


def device_at(orient, layer, spot):
    if orient == 0:
        return (layer << 5) + spot
    if orient == 1:
        return ((spot >> 3) << 5) + (layer << 3) + (spot & 7)
    return ((spot >> 1) << 3) + (layer << 1) + (spot & 1)


def shifted(spot, step):
    a = ((spot >> 3) + (step >> 3)) & 3
    b = ((spot >> 1) + (step >> 1)) & 3
    return (a << 3) + (b << 1) + ((spot + step) & 1)


def remote(src, dst, send, recv, device):
    return pltpu.make_async_remote_copy(
        src_ref=src, dst_ref=dst, send_sem=send, recv_sem=recv, device_id=(device,), device_id_type=MESH
    )


def unit_rows(values):
    total = jnp.sum(values * values, axis=-1, keepdims=True)
    return (values * lax.rsqrt(total + EPS)).astype(jnp.bfloat16)


def code_rows(codes):
    values = codes.astype(jnp.bfloat16).astype(jnp.float32)
    inverse = lax.rsqrt(jnp.sum(values * values, axis=-1, keepdims=True) + EPS)
    return (values * inverse).astype(jnp.bfloat16), inverse


def back_norm(grad, code_unit, inverse):
    values = code_unit.astype(jnp.float32)
    return (grad - values * jnp.sum(values * grad, axis=-1, keepdims=True)) * inverse


def dot(a, b, dims=((1,), (0,))):
    return lax.dot_general(a, b, (dims, ((), ())), preferred_element_type=jnp.float32)


def digit_sum(place_sum, step):
    return ((((place_sum >> 2) + (step >> 2)) & 3) << 2) + ((place_sum + step) & 3)


WAVE = 4
SPLIT = ((1, 16), (4, 4), (16, 1))
GREETED = [(0, step) for step in range(1, 32)] + [(1, step) for step in range(8, 32)]
GREETED += [(2, step) for step in range(8, 32) if (step >> 1) & 3]
GREETED.sort(key=lambda at: -(min(at[1] >> 3, 4 - (at[1] >> 3)) + min((at[1] >> 1) & 3, 4 - ((at[1] >> 1) & 3))))


def step_kernel(
    nb_hbm, teacher_hbm, weight_hbm, head_ref, grad_ref,
    table_ref, tablev_ref, nbv_ref, teacher_ref, weight_ref, unit_ref, both_ref, code_ref, tcode_ref, inv_ref, self_ref,
    perm_ref, swap_ref, member_ref, stage, held0, held1, held2, picked0, picked1, wide0, wide1, tall_ref, product0, product1,
    mixed_ref, share_ref,
    cross_out, cross_in, part_out, part_in,
    out0, out1, out2, mid0, mid1, mid2, sum0, sum1, sum2, in0, in1, in2, tail_out, tail_in,
    load_sem, own_sem, *sems,
):
    held, share_out, share_mid = (held0, held1, held2), (out0, out1, out2), (mid0, mid1, mid2)
    share_sum, layer_in = (sum0, sum1, sum2), (in0, in1, in2)
    pairs = [(sems[2 * i], sems[2 * i + 1]) for i in range(len(sems) // 2)]
    deal_sem, layer_sem, serve0_sem, serve1_sem, cross_sem, part_sem, core_sem, axis_sem, tail_sem = pairs
    waves = (
        (0, WAVE, picked0, wide0, product0, serve0_sem),
        (WAVE, KNN, picked1, wide1, product1, serve1_sem),
    )
    me = lax.axis_index("dp")
    where = [place(o, me) for o in range(3)]
    core = me & 1
    barrier = pltpu.get_barrier_semaphore()
    loads = [
        pltpu.make_async_copy(teacher_hbm.at[0], teacher_ref, load_sem.at[0]),
        pltpu.make_async_copy(weight_hbm, weight_ref, load_sem.at[1]),
        pltpu.make_async_copy(nb_hbm, nbv_ref, load_sem.at[2]),
    ]
    for load in loads:
        load.start()

    for o, step in GREETED:
        layer, spot = where[o]
        pl.semaphore_signal(barrier, inc=1, device_id=(device_at(o, layer, shifted(spot, step)),), device_id_type=MESH)
    loads[0].wait()
    values = unit_rows(teacher_ref[...].astype(jnp.float32))
    unit_ref[...] = values
    tall_ref[...] = jnp.transpose(values.astype(jnp.float32)).astype(jnp.bfloat16)
    for load in loads[1:]:
        load.wait()
    named = nbv_ref[...]
    for o in range(3):
        up, at = place(o, named)
        tablev_ref[o, 0:KNN, :] = (up << 5) + ((at & 1) << 4) + (at >> 1)
        tablev_ref[o, KNN:8, :] = jnp.zeros((2, 128), jnp.int32)
    table_load = pltpu.make_async_copy(tablev_ref, table_ref, load_sem.at[3])
    table_load.start()
    table_load.wait()
    pl.semaphore_wait(barrier, len(GREETED))

    def tile(o, at):
        return tall_ref.at[pl.ds(pl.multiple_of(512 * o + at * 32, 32), 32)]

    own = []
    for o in range(3):
        layer, spot = where[o]
        at = spot >> 1

        def deal(step, carry):
            to = digit_sum(at, step)
            remote(
                tile(o, to), stage.at[o, at], deal_sem[0].at[o], deal_sem[1].at[o],
                device_at(o, layer, (to << 1) + core),
            ).start()
            return carry

        lax.fori_loop(1, 16, deal, 0)
        own.append(pltpu.make_async_copy(tile(o, at), stage.at[o, at], own_sem.at[o]))
        own[o].start()

    code_unit, inverse = code_rows(dot(unit_ref[...], weight_ref[...]))
    code_ref[...] = code_unit
    inv_ref[...] = jnp.broadcast_to(inverse, inv_ref.shape)

    for o in range(3):
        layer, spot = where[o]
        own[o].wait()
        part = stage.at[o, pl.ds(0, 15)]
        remote(part, part, deal_sem[0].at[o], deal_sem[1].at[o], me).wait()
        mine = held[o].at[pl.ds((layer * 2 + core) * 16, 16)]
        for hop in range(1, 8):
            up, side = (layer + (hop >> 1)) & 3, (core + hop) & 1
            remote(
                stage.at[o, :, pl.ds(pl.multiple_of(side * 16, 16), 16)], mine, layer_sem[0].at[o], layer_sem[1].at[o],
                device_at(o, up, spot - core + side),
            ).start()
        own[o] = pltpu.make_async_copy(stage.at[o, :, pl.ds(pl.multiple_of(core * 16, 16), 16)], mine, own_sem.at[o])
        own[o].start()

    units, codes = unit_ref[...], code_ref[...]
    tcorr = dot(units, units, ((1,), (1,)))
    scor = dot(codes, codes, ((1,), (1,)))
    gate = (-(LOSS_SCALE * WEIGHT_SELF) * (tcorr - SHIFT_SELF) * jnp.maximum(scor, 0.0)).astype(jnp.bfloat16)
    self_ref[...] = dot(gate, codes) + dot(gate, codes, ((0,), (0,)))

    both_ref[0:384, :] = jnp.transpose(weight_ref[...].astype(jnp.float32)).astype(jnp.bfloat16)
    both_ref[384:512, :] = units
    tcode_ref[...] = jnp.transpose(codes.astype(jnp.float32)).astype(jnp.bfloat16)
    row = lax.broadcasted_iota(jnp.int32, (768, 128), 0)
    col = lax.broadcasted_iota(jnp.int32, (768, 128), 1)
    block = (row * 2731) >> 16
    within = jnp.where(block == (col >> 2), row - 24 * block - (col & 3), -1)
    for k in range(KNN):
        perm_ref[:, 128 * k : 128 * (k + 1)] = jnp.where(within == 4 * k, 1.0, 0.0).astype(jnp.bfloat16)
    row = lax.broadcasted_iota(jnp.int32, (128, 128), 0)
    col = lax.broadcasted_iota(jnp.int32, (128, 128), 1)
    swap_ref[...] = jnp.where(
        col == (((row >> 2) & 1) << 6) + ((row >> 3) << 2) + (row & 3), 1.0, 0.0
    ).astype(jnp.bfloat16)

    spans = []
    for o in range(3):
        layer, spot = where[o]
        own[o].wait()
        part = held[o].at[pl.ds(0, 7 * 16)]
        remote(part, part, layer_sem[0].at[o], layer_sem[1].at[o], me).wait()
        spans.append(pl.ds(pl.multiple_of(512 * o + spot * 16, 16), 16))

    for first, last, picked, wide, _, sem in waves:

        def pick(o, step):
            layer, spot = where[o]
            asker = device_at(o, layer, shifted(spot, step))
            for k in range(first, last):
                lanes = slice(128 * (k - first), 128 * (k - first + 1))
                picked[o, step, :, lanes] = held[o][table_ref[o, k, asker]]
            return asker

        def serve(step, carry):
            for o in range(3):
                asker = pick(o, step)
                remote(picked.at[o, step], wide.at[spans[o]], sem[0].at[o], sem[1].at[o], asker).start()
            return carry

        lax.fori_loop(1, RING, serve, 0)
        for o in range(3):
            pick(o, 0)
            pltpu.make_async_copy(picked.at[o, 0], wide.at[spans[o]], own_sem.at[o + (3 if first else 0)]).start()

    slots = nbv_ref[...].astype(jnp.float32).astype(jnp.bfloat16)
    col = lax.broadcasted_iota(jnp.int32, (1, 768), 1)
    source = (col * 2731) >> 16
    slot_of = (col - 24 * source) >> 2
    mine = lax.broadcasted_iota(jnp.int32, (KNN, 768), 0) == slot_of
    image = lax.broadcasted_iota(jnp.int32, (128, 768), 0)
    row = lax.broadcasted_iota(jnp.int32, (512, 128), 0)
    same = (row & 3) == (lax.broadcasted_iota(jnp.int32, (512, 128), 1) & 3)
    for o in range(3):
        layer, spot = where[o]
        chosen = jnp.where(image == device_at(o, layer, source), 1.0, 0.0).astype(jnp.bfloat16)
        named = jnp.sum(jnp.where(mine, dot(slots, chosen), 0.0), axis=0, keepdims=True)
        owner = device_at(o, row >> 7, (((row >> 2) & 15) << 1) + ((row >> 6) & 1))
        owner = jnp.where(same, owner, -1).astype(jnp.float32)
        for k in range(KNN):
            lanes = slice(128 * k, 128 * (k + 1))
            member_ref[o, :, lanes] = jnp.where(owner == named[:, lanes], 1.0, 0.0).astype(jnp.bfloat16)

    for first, last, picked, wide, product_ref, sem in waves:
        for o in range(3):
            pltpu.make_async_copy(picked.at[o, 0], picked.at[o, 0], own_sem.at[o + (3 if first else 0)]).wait()
            part = picked.at[o, pl.ds(1, RING - 1)]
            remote(part, part, sem[0].at[o], sem[1].at[o], me).wait()
            third = slice(512 * o, 512 * (o + 1))
            product = dot(both_ref[:, third], wide[third, :])
            product_ref[...] = product if o == 0 else product_ref[...] + product

        values = product_ref[0:384, :].astype(jnp.bfloat16).astype(jnp.float32)
        partner_inv = lax.rsqrt(jnp.sum(values * values, axis=0, keepdims=True) + EPS)
        partner_code = (values * partner_inv).astype(jnp.bfloat16)
        tcorr = product_ref[384:512, :]
        scor = dot(code_ref[...], partner_code)
        gate = (-(LOSS_SCALE * WEIGHT_PAIR) * (tcorr - SHIFT_PAIR) * jnp.maximum(scor, 0.0)).astype(jnp.bfloat16)
        raw = dot(tcode_ref[...], gate)
        values = partner_code.astype(jnp.float32)
        cross = ((raw - values * jnp.sum(values * raw, axis=0, keepdims=True)) * partner_inv).astype(jnp.bfloat16)
        mixed = dot(perm_ref[:, 128 * first : 128 * last], cross, ((1,), (1,)))
        if first == 0:
            mixed_ref[...] = mixed
            self_ref[...] = self_ref[...] + dot(gate, partner_code, ((1,), (1,)))
            share_ref[0:1536, :] = dot(wide[...], cross, ((1,), (1,)))
        else:
            cross_out[...] = (mixed_ref[...] + mixed).reshape(RING, 24, 384).astype(jnp.bfloat16)

    def give(step, carry):
        for o in range(3):
            layer, spot = where[o]
            target = shifted(spot, step)
            remote(
                cross_out.at[target, :, pl.ds(128 * o, 128)], cross_in.at[o, spot], cross_sem[0].at[o], cross_sem[1].at[o],
                device_at(o, layer, target),
            ).start()
        return carry

    lax.fori_loop(1, RING, give, 0)
    for o in range(3):
        spot = where[o][1]
        cross_in[o, spot] = cross_out[spot, :, 128 * o : 128 * (o + 1)]

    grad = self_ref[...] + dot(gate, partner_code, ((1,), (1,)))
    own_grad = back_norm(grad, code_ref[...], inv_ref[:, 0:1])
    self_ref[...] = own_grad

    coarse = own_grad.astype(jnp.bfloat16)
    fine = (own_grad - coarse.astype(jnp.float32)).astype(jnp.bfloat16)
    share_ref[0:1536, :] = share_ref[0:1536, :] + (
        dot(wide1[...], cross, ((1,), (1,))) + dot(tall_ref[...], coarse) + dot(tall_ref[...], fine)
    )

    def cut(chip, carry):
        first = share_ref[pl.ds(pl.multiple_of(chip * 24, 8), 16), :].astype(jnp.bfloat16)
        second = share_ref[pl.ds(pl.multiple_of(chip * 24 + 8, 8), 24), :][4:20].astype(jnp.bfloat16)
        for o, at in enumerate(((0, chip >> 4, chip & 15), (chip >> 4, (chip >> 2) & 3, chip & 3), (chip >> 2, chip & 3, 0))):
            share_out[o][0, at[0], at[1], at[2]] = first[:, 128 * o : 128 * (o + 1)]
            share_out[o][1, at[0], at[1], at[2]] = second[:, 128 * o : 128 * (o + 1)]
        return carry

    lax.fori_loop(0, 64, cut, 0)
    for o in range(3):
        remote(share_out[o].at[1 - core], share_mid[o], core_sem[0].at[o], core_sem[1].at[o], me + 1 - 2 * core).start()

    for o in range(3):
        layer, spot = where[o]
        remote(share_out[o].at[0], share_mid[o], core_sem[0].at[o], core_sem[1].at[o], me).wait()
        total = share_out[o][core].astype(jnp.float32) + share_mid[o][...].astype(jnp.float32)
        share_sum[o][...] = total.astype(jnp.bfloat16)
        for hop in range(1, SIDE):
            to = (layer + hop) & 3
            remote(
                share_sum[o].at[:, to], layer_in[o].at[layer], axis_sem[0].at[o], axis_sem[1].at[o], device_at(o, to, spot)
            ).start()
        layer_in[o][layer] = share_sum[o][:, layer]

    for o in range(3):
        layer, spot = where[o]
        part = cross_in.at[o, pl.ds(0, RING - 1)]
        remote(part, part, cross_sem[0].at[o], cross_sem[1].at[o], me).wait()
        piece = dot(member_ref[o], cross_in[o].reshape(768, 128))
        part_out[o] = piece.astype(jnp.bfloat16).reshape(8, 64, 128)
        mine = layer * 2 + core
        for hop in range(1, 8):
            up, side = (layer + (hop >> 1)) & 3, (core + hop) & 1
            remote(
                part_out.at[o, up * 2 + side], part_in.at[o, mine], part_sem[0].at[o], part_sem[1].at[o],
                device_at(o, up, spot - core + side),
            ).start()
        part_in[o, mine] = part_out[o, mine]

    for o in range(3):
        layer, spot = where[o]
        at = spot >> 1
        part = part_in.at[o, pl.ds(0, 7)]
        remote(part, part, part_sem[0].at[o], part_sem[1].at[o], me).wait()
        relayed = jnp.sum(part_in[o].reshape(4, 128, 128).astype(jnp.float32), axis=0).astype(jnp.bfloat16)
        tail_out[o, :, 16:24] = dot(swap_ref[...], relayed).reshape(16, 8, 128).astype(jnp.bfloat16)
        part = layer_in[o].at[pl.ds(0, SIDE - 1)]
        remote(part, part, axis_sem[0].at[o], axis_sem[1].at[o], me).wait()
        total = jnp.sum(layer_in[o][...].astype(jnp.float32), axis=0)
        tail_out[o, :, 0:16] = total.astype(jnp.bfloat16).reshape(16, 16, 128)

        def finish(step, carry):
            to = digit_sum(at, step)
            remote(
                tail_out.at[o, to], tail_in.at[o, at], tail_sem[0].at[o], tail_sem[1].at[o],
                device_at(o, layer, (to << 1) + core),
            ).start()
            return carry

        lax.fori_loop(1, 16, finish, 0)
        tail_in[o, at] = tail_out[o, at]

    for o in range(3):
        lanes = slice(128 * o, 128 * (o + 1))
        part = tail_in.at[o, pl.ds(0, 15)]
        remote(part, part, tail_sem[0].at[o], tail_sem[1].at[o], me).wait()
        relayed = tail_in[o, :, 16:24].astype(jnp.float32).reshape(128, 128)
        grad_ref[0, :, lanes] = self_ref[:, lanes] + relayed
        total = jnp.sum(tail_in[o, :, 0:16].astype(jnp.float32), axis=0)
        head_ref[:, lanes] = total[0:12]


def body(teacher, head_weight, neighbours):
    vmem = pl.BlockSpec(memory_space=pltpu.VMEM)
    hbm = pl.BlockSpec(memory_space=pl.ANY)
    half, full = jnp.bfloat16, jnp.float32
    return pl.pallas_call(
        step_kernel,
        out_shape=(jax.ShapeDtypeStruct((12, 384), full), jax.ShapeDtypeStruct((1, 128, 384), full)),
        in_specs=[hbm, hbm, hbm],
        out_specs=(vmem, vmem),
        scratch_shapes=[
            pltpu.SMEM((3, 8, 128), jnp.int32),
            pltpu.VMEM((3, 8, 128), jnp.int32),
            pltpu.VMEM((KNN, 128), jnp.int32),
            pltpu.VMEM((128, 1536), half),
            pltpu.VMEM((1536, 384), half),
            pltpu.VMEM((128, 1536), half),
            pltpu.VMEM((512, 1536), half),
            pltpu.VMEM((128, 384), half),
            pltpu.VMEM((384, 128), half),
            pltpu.VMEM((128, 128), full),
            pltpu.VMEM((128, 384), full),
            pltpu.VMEM((768, 768), half),
            pltpu.VMEM((128, 128), half),
            pltpu.VMEM((3, 512, 768), half),
            pltpu.VMEM((3, 16, 32, 128), half),
        ]
        + [pltpu.VMEM((128, 16, 128), half)] * 3
        + [
            pltpu.VMEM((3, RING, 16, WAVE * 128), half),
            pltpu.VMEM((3, RING, 16, (KNN - WAVE) * 128), half),
            pltpu.VMEM((1536, WAVE * 128), half),
            pltpu.VMEM((1536, (KNN - WAVE) * 128), half),
            pltpu.VMEM((1536, 128), half),
            pltpu.VMEM((512, WAVE * 128), full),
            pltpu.VMEM((512, (KNN - WAVE) * 128), full),
            pltpu.VMEM((768, 384), full),
            pltpu.VMEM((1544, 384), full),
            pltpu.VMEM((RING, 24, 384), half),
            pltpu.VMEM((3, RING, 24, 128), half),
            pltpu.VMEM((3, 8, 64, 128), half),
            pltpu.VMEM((3, 8, 64, 128), half),
        ]
        + [pltpu.VMEM((2, a, 4, b, 16, 128), half) for a, b in SPLIT]
        + [pltpu.VMEM((a, 4, b, 16, 128), half) for a, b in SPLIT] * 2
        + [pltpu.VMEM((4, a, b, 16, 128), half) for a, b in SPLIT]
        + [pltpu.VMEM((3, 16, 24, 128), half)] * 2
        + [pltpu.SemaphoreType.DMA((4,)), pltpu.SemaphoreType.DMA((6,))]
        + [pltpu.SemaphoreType.DMA((3,))] * 18,
        compiler_params=pltpu.CompilerParams(
            collective_id=0, has_side_effects=True, vmem_limit_bytes=(65536 - 10752) * 1024
        ),
    )(jnp.transpose(neighbours), teacher, head_weight)


def solution(mesh):
    return jax.shard_map(
        body,
        mesh=mesh,
        in_specs=(P("dp", None, None), P(), P()),
        out_specs=(P("dp", None), P("dp", None, None)),
        check_vma=False,
    )
```

```python
import jax
import jax.numpy as jnp
from jax import lax
from jax.experimental import pallas as pl
from jax.experimental.pallas import tpu as pltpu
from jax.sharding import PartitionSpec as P

EPS = 1e-06
LOSS_SCALE = 128.0
SHIFT_SELF = 0.18
WEIGHT_SELF = 0.1
SHIFT_PAIR = 0.12
WEIGHT_PAIR = 0.5
MESH = pl.DeviceIdType.MESH
SIDE = 4
RING = 32
KNN = 6


def place(orient, index):
    y, x, z, c = index >> 5, (index >> 3) & 3, (index >> 1) & 3, index & 1
    if orient == 0:
        return y, index & 31
    if orient == 1:
        return x, (y << 3) + (index & 7)
    return z, ((index >> 3) << 1) + c


def device_at(orient, layer, spot):
    if orient == 0:
        return (layer << 5) + spot
    if orient == 1:
        return ((spot >> 3) << 5) + (layer << 3) + (spot & 7)
    return ((spot >> 1) << 3) + (layer << 1) + (spot & 1)


def shifted(spot, step):
    a = ((spot >> 3) + (step >> 3)) & 3
    b = ((spot >> 1) + (step >> 1)) & 3
    return (a << 3) + (b << 1) + ((spot + step) & 1)


def remote(src, dst, send, recv, device):
    return pltpu.make_async_remote_copy(
        src_ref=src, dst_ref=dst, send_sem=send, recv_sem=recv, device_id=(device,), device_id_type=MESH
    )


def unit_rows(values):
    total = jnp.sum(values * values, axis=-1, keepdims=True)
    return (values * lax.rsqrt(total + EPS)).astype(jnp.bfloat16)


def code_rows(codes):
    values = codes.astype(jnp.bfloat16).astype(jnp.float32)
    inverse = lax.rsqrt(jnp.sum(values * values, axis=-1, keepdims=True) + EPS)
    return (values * inverse).astype(jnp.bfloat16), inverse


def back_norm(grad, code_unit, inverse):
    values = code_unit.astype(jnp.float32)
    return (grad - values * jnp.sum(values * grad, axis=-1, keepdims=True)) * inverse


def dot(a, b, dims=((1,), (0,))):
    return lax.dot_general(a, b, (dims, ((), ())), preferred_element_type=jnp.float32)


def digit_sum(place_sum, step):
    return ((((place_sum >> 2) + (step >> 2)) & 3) << 2) + ((place_sum + step) & 3)


WAVE = 4
FAR1 = sorted(range(1, 16), key=lambda step: -(min(step >> 2, 4 - (step >> 2)) + min(step & 3, 4 - (step & 3))))
FAR2 = sorted(range(1, 32), key=lambda step: -(min(step >> 3, 4 - (step >> 3)) + min((step >> 1) & 3, 4 - ((step >> 1) & 3))))
SPLIT = ((1, 16), (4, 4), (16, 1))
GREETED = [(0, step) for step in range(1, 32)] + [(1, step) for step in range(8, 32)]
GREETED += [(2, step) for step in range(8, 32) if (step >> 1) & 3]
GREETED.sort(key=lambda at: -(min(at[1] >> 3, 4 - (at[1] >> 3)) + min((at[1] >> 1) & 3, 4 - ((at[1] >> 1) & 3))))


def step_kernel(
    nb_hbm, teacher_hbm, weight_hbm, head_ref, grad_ref,
    table_ref, tablev_ref, nbv_ref, teacher_ref, weight_ref, unit_ref, both_ref, code_ref, tcode_ref, inv_ref, self_ref,
    perm_ref, swap_ref, member_ref, stage, held0, held1, held2, picked0, picked1, wide0, wide1, tall_ref, product0, product1,
    mixed_ref, share_ref,
    cross_out, cross_in, part_out, part_in,
    out0, out1, out2, mid0, mid1, mid2, sum0, sum1, sum2, in0, in1, in2, tail_out, tail_in,
    load_sem, own_sem, *sems,
):
    held, share_out, share_mid = (held0, held1, held2), (out0, out1, out2), (mid0, mid1, mid2)
    share_sum, layer_in = (sum0, sum1, sum2), (in0, in1, in2)
    pairs = [(sems[2 * i], sems[2 * i + 1]) for i in range(len(sems) // 2)]
    deal_sem, layer_sem, serve0_sem, serve1_sem, cross_sem, part_sem, core_sem, axis_sem, tail_sem = pairs
    waves = (
        (0, WAVE, picked0, wide0, product0, serve0_sem),
        (WAVE, KNN, picked1, wide1, product1, serve1_sem),
    )
    me = lax.axis_index("dp")
    where = [place(o, me) for o in range(3)]
    core = me & 1
    barrier = pltpu.get_barrier_semaphore()
    loads = [
        pltpu.make_async_copy(teacher_hbm.at[0], teacher_ref, load_sem.at[0]),
        pltpu.make_async_copy(weight_hbm, weight_ref, load_sem.at[1]),
        pltpu.make_async_copy(nb_hbm, nbv_ref, load_sem.at[2]),
    ]
    for load in loads:
        load.start()

    for o, step in GREETED:
        layer, spot = where[o]
        pl.semaphore_signal(barrier, inc=1, device_id=(device_at(o, layer, shifted(spot, step)),), device_id_type=MESH)
    loads[0].wait()
    values = unit_rows(teacher_ref[...].astype(jnp.float32))
    unit_ref[...] = values
    tall_ref[...] = jnp.transpose(values.astype(jnp.float32)).astype(jnp.bfloat16)
    for load in loads[1:]:
        load.wait()
    named = nbv_ref[...]
    for o in range(3):
        up, at = place(o, named)
        tablev_ref[o, 0:KNN, :] = (up << 5) + ((at & 1) << 4) + (at >> 1)
        tablev_ref[o, KNN:8, :] = jnp.zeros((2, 128), jnp.int32)
    table_load = pltpu.make_async_copy(tablev_ref, table_ref, load_sem.at[3])
    table_load.start()
    table_load.wait()
    pl.semaphore_wait(barrier, len(GREETED))

    def tile(o, at):
        return tall_ref.at[pl.ds(pl.multiple_of(512 * o + at * 32, 32), 32)]

    own = []
    for o in range(3):
        layer, spot = where[o]
        at = spot >> 1

        def deal(step, carry):
            to = digit_sum(at, step)
            remote(
                tile(o, to), stage.at[o, at], deal_sem[0].at[o], deal_sem[1].at[o],
                device_at(o, layer, (to << 1) + core),
            ).start()
            return carry

        for step in FAR1:
            deal(step, 0)
        own.append(pltpu.make_async_copy(tile(o, at), stage.at[o, at], own_sem.at[o]))
        own[o].start()

    code_unit, inverse = code_rows(dot(unit_ref[...], weight_ref[...]))
    code_ref[...] = code_unit
    inv_ref[...] = jnp.broadcast_to(inverse, inv_ref.shape)

    for o in range(3):
        layer, spot = where[o]
        own[o].wait()
        part = stage.at[o, pl.ds(0, 15)]
        remote(part, part, deal_sem[0].at[o], deal_sem[1].at[o], me).wait()
        mine = held[o].at[pl.ds((layer * 2 + core) * 16, 16)]
        for hop in (4, 5, 2, 3, 6, 7, 1):
            up, side = (layer + (hop >> 1)) & 3, (core + hop) & 1
            remote(
                stage.at[o, :, pl.ds(pl.multiple_of(side * 16, 16), 16)], mine, layer_sem[0].at[o], layer_sem[1].at[o],
                device_at(o, up, spot - core + side),
            ).start()
        own[o] = pltpu.make_async_copy(stage.at[o, :, pl.ds(pl.multiple_of(core * 16, 16), 16)], mine, own_sem.at[o])
        own[o].start()

    units, codes = unit_ref[...], code_ref[...]
    tcorr = dot(units, units, ((1,), (1,)))
    scor = dot(codes, codes, ((1,), (1,)))
    gate = (-(LOSS_SCALE * WEIGHT_SELF) * (tcorr - SHIFT_SELF) * jnp.maximum(scor, 0.0)).astype(jnp.bfloat16)
    self_ref[...] = dot(gate, codes) + dot(gate, codes, ((0,), (0,)))

    both_ref[0:384, :] = jnp.transpose(weight_ref[...].astype(jnp.float32)).astype(jnp.bfloat16)
    both_ref[384:512, :] = units
    tcode_ref[...] = jnp.transpose(codes.astype(jnp.float32)).astype(jnp.bfloat16)
    row = lax.broadcasted_iota(jnp.int32, (768, 128), 0)
    col = lax.broadcasted_iota(jnp.int32, (768, 128), 1)
    block = (row * 2731) >> 16
    within = jnp.where(block == (col >> 2), row - 24 * block - (col & 3), -1)
    for k in range(KNN):
        perm_ref[:, 128 * k : 128 * (k + 1)] = jnp.where(within == 4 * k, 1.0, 0.0).astype(jnp.bfloat16)
    row = lax.broadcasted_iota(jnp.int32, (128, 128), 0)
    col = lax.broadcasted_iota(jnp.int32, (128, 128), 1)
    swap_ref[...] = jnp.where(
        col == (((row >> 2) & 1) << 6) + ((row >> 3) << 2) + (row & 3), 1.0, 0.0
    ).astype(jnp.bfloat16)

    spans = []
    for o in range(3):
        layer, spot = where[o]
        own[o].wait()
        part = held[o].at[pl.ds(0, 7 * 16)]
        remote(part, part, layer_sem[0].at[o], layer_sem[1].at[o], me).wait()
        spans.append(pl.ds(pl.multiple_of(512 * o + spot * 16, 16), 16))

    for first, last, picked, wide, _, sem in waves:

        def pick(o, step):
            layer, spot = where[o]
            asker = device_at(o, layer, shifted(spot, step))
            for k in range(first, last):
                lanes = slice(128 * (k - first), 128 * (k - first + 1))
                picked[o, step, :, lanes] = held[o][table_ref[o, k, asker]]
            return asker

        def serve(step, carry):
            for o in range(3):
                asker = pick(o, step)
                remote(picked.at[o, step], wide.at[spans[o]], sem[0].at[o], sem[1].at[o], asker).start()
            return carry

        lax.fori_loop(1, RING, serve, 0)
        for o in range(3):
            pick(o, 0)
            pltpu.make_async_copy(picked.at[o, 0], wide.at[spans[o]], own_sem.at[o + (3 if first else 0)]).start()

    slots = nbv_ref[...].astype(jnp.float32).astype(jnp.bfloat16)
    col = lax.broadcasted_iota(jnp.int32, (1, 768), 1)
    source = (col * 2731) >> 16
    slot_of = (col - 24 * source) >> 2
    mine = lax.broadcasted_iota(jnp.int32, (KNN, 768), 0) == slot_of
    image = lax.broadcasted_iota(jnp.int32, (128, 768), 0)
    row = lax.broadcasted_iota(jnp.int32, (512, 128), 0)
    same = (row & 3) == (lax.broadcasted_iota(jnp.int32, (512, 128), 1) & 3)
    for o in range(3):
        layer, spot = where[o]
        chosen = jnp.where(image == device_at(o, layer, source), 1.0, 0.0).astype(jnp.bfloat16)
        named = jnp.sum(jnp.where(mine, dot(slots, chosen), 0.0), axis=0, keepdims=True)
        owner = device_at(o, row >> 7, (((row >> 2) & 15) << 1) + ((row >> 6) & 1))
        owner = jnp.where(same, owner, -1).astype(jnp.float32)
        for k in range(KNN):
            lanes = slice(128 * k, 128 * (k + 1))
            member_ref[o, :, lanes] = jnp.where(owner == named[:, lanes], 1.0, 0.0).astype(jnp.bfloat16)

    for first, last, picked, wide, product_ref, sem in waves:
        for o in range(3):
            pltpu.make_async_copy(picked.at[o, 0], picked.at[o, 0], own_sem.at[o + (3 if first else 0)]).wait()
            part = picked.at[o, pl.ds(1, RING - 1)]
            remote(part, part, sem[0].at[o], sem[1].at[o], me).wait()
            third = slice(512 * o, 512 * (o + 1))
            product = dot(both_ref[:, third], wide[third, :])
            product_ref[...] = product if o == 0 else product_ref[...] + product

        values = product_ref[0:384, :].astype(jnp.bfloat16).astype(jnp.float32)
        partner_inv = lax.rsqrt(jnp.sum(values * values, axis=0, keepdims=True) + EPS)
        partner_code = (values * partner_inv).astype(jnp.bfloat16)
        tcorr = product_ref[384:512, :]
        scor = dot(code_ref[...], partner_code)
        gate = (-(LOSS_SCALE * WEIGHT_PAIR) * (tcorr - SHIFT_PAIR) * jnp.maximum(scor, 0.0)).astype(jnp.bfloat16)
        raw = dot(tcode_ref[...], gate)
        values = partner_code.astype(jnp.float32)
        cross = ((raw - values * jnp.sum(values * raw, axis=0, keepdims=True)) * partner_inv).astype(jnp.bfloat16)
        mixed = dot(perm_ref[:, 128 * first : 128 * last], cross, ((1,), (1,)))
        if first == 0:
            mixed_ref[...] = mixed
            self_ref[...] = self_ref[...] + dot(gate, partner_code, ((1,), (1,)))
            share_ref[0:1536, :] = dot(wide[...], cross, ((1,), (1,)))
        else:
            cross_out[...] = (mixed_ref[...] + mixed).reshape(RING, 24, 384).astype(jnp.bfloat16)

    def give(step, carry):
        for o in range(3):
            layer, spot = where[o]
            target = shifted(spot, step)
            remote(
                cross_out.at[target, :, pl.ds(128 * o, 128)], cross_in.at[o, spot], cross_sem[0].at[o], cross_sem[1].at[o],
                device_at(o, layer, target),
            ).start()
        return carry

    for step in FAR2:
        give(step, 0)
    for o in range(3):
        spot = where[o][1]
        cross_in[o, spot] = cross_out[spot, :, 128 * o : 128 * (o + 1)]

    grad = self_ref[...] + dot(gate, partner_code, ((1,), (1,)))
    own_grad = back_norm(grad, code_ref[...], inv_ref[:, 0:1])
    self_ref[...] = own_grad

    coarse = own_grad.astype(jnp.bfloat16)
    fine = (own_grad - coarse.astype(jnp.float32)).astype(jnp.bfloat16)
    share_ref[0:1536, :] = share_ref[0:1536, :] + (
        dot(wide1[...], cross, ((1,), (1,))) + dot(tall_ref[...], coarse) + dot(tall_ref[...], fine)
    )

    for o in range(3):
        lanes = slice(128 * o, 128 * (o + 1))

        def cut(chip, carry):
            a, b, c = ((0, chip >> 4, chip & 15), (chip >> 4, (chip >> 2) & 3, chip & 3), (chip >> 2, chip & 3, 0))[o]
            first = share_ref[pl.ds(pl.multiple_of(chip * 24, 8), 16), lanes]
            second = share_ref[pl.ds(pl.multiple_of(chip * 24 + 8, 8), 24), lanes][4:20]
            share_out[o][0, a, b, c] = first.astype(jnp.bfloat16)
            share_out[o][1, a, b, c] = second.astype(jnp.bfloat16)
            return carry

        lax.fori_loop(0, 64, cut, 0)
        remote(share_out[o].at[1 - core], share_mid[o], core_sem[0].at[o], core_sem[1].at[o], me + 1 - 2 * core).start()

    for o in range(3):
        layer, spot = where[o]
        remote(share_out[o].at[0], share_mid[o], core_sem[0].at[o], core_sem[1].at[o], me).wait()
        total = share_out[o][core].astype(jnp.float32) + share_mid[o][...].astype(jnp.float32)
        share_sum[o][...] = total.astype(jnp.bfloat16)
        for hop in (2, 1, 3):
            to = (layer + hop) & 3
            remote(
                share_sum[o].at[:, to], layer_in[o].at[layer], axis_sem[0].at[o], axis_sem[1].at[o], device_at(o, to, spot)
            ).start()
        layer_in[o][layer] = share_sum[o][:, layer]

    for o in range(3):
        layer, spot = where[o]
        part = cross_in.at[o, pl.ds(0, RING - 1)]
        remote(part, part, cross_sem[0].at[o], cross_sem[1].at[o], me).wait()
        piece = dot(member_ref[o], cross_in[o].reshape(768, 128))
        part_out[o] = piece.astype(jnp.bfloat16).reshape(8, 64, 128)
        mine = layer * 2 + core
        for hop in (4, 5, 2, 3, 6, 7, 1):
            up, side = (layer + (hop >> 1)) & 3, (core + hop) & 1
            remote(
                part_out.at[o, up * 2 + side], part_in.at[o, mine], part_sem[0].at[o], part_sem[1].at[o],
                device_at(o, up, spot - core + side),
            ).start()
        part_in[o, mine] = part_out[o, mine]

    for o in range(3):
        layer, spot = where[o]
        at = spot >> 1
        part = part_in.at[o, pl.ds(0, 7)]
        remote(part, part, part_sem[0].at[o], part_sem[1].at[o], me).wait()
        relayed = jnp.sum(part_in[o].reshape(4, 128, 128).astype(jnp.float32), axis=0).astype(jnp.bfloat16)
        tail_out[o, :, 16:24] = dot(swap_ref[...], relayed).reshape(16, 8, 128).astype(jnp.bfloat16)
        part = layer_in[o].at[pl.ds(0, SIDE - 1)]
        remote(part, part, axis_sem[0].at[o], axis_sem[1].at[o], me).wait()
        total = jnp.sum(layer_in[o][...].astype(jnp.float32), axis=0)
        tail_out[o, :, 0:16] = total.astype(jnp.bfloat16).reshape(16, 16, 128)

        def finish(step, carry):
            to = digit_sum(at, step)
            remote(
                tail_out.at[o, to], tail_in.at[o, at], tail_sem[0].at[o], tail_sem[1].at[o],
                device_at(o, layer, (to << 1) + core),
            ).start()
            return carry

        for step in FAR1:
            finish(step, 0)
        tail_in[o, at] = tail_out[o, at]

    for o in range(3):
        lanes = slice(128 * o, 128 * (o + 1))
        part = tail_in.at[o, pl.ds(0, 15)]
        remote(part, part, tail_sem[0].at[o], tail_sem[1].at[o], me).wait()
        relayed = tail_in[o, :, 16:24].astype(jnp.float32).reshape(128, 128)
        grad_ref[0, :, lanes] = self_ref[:, lanes] + relayed
        total = jnp.sum(tail_in[o, :, 0:16].astype(jnp.float32), axis=0)
        head_ref[:, lanes] = total[0:12]


def body(teacher, head_weight, neighbours):
    vmem = pl.BlockSpec(memory_space=pltpu.VMEM)
    hbm = pl.BlockSpec(memory_space=pl.ANY)
    half, full = jnp.bfloat16, jnp.float32
    return pl.pallas_call(
        step_kernel,
        out_shape=(jax.ShapeDtypeStruct((12, 384), full), jax.ShapeDtypeStruct((1, 128, 384), full)),
        in_specs=[hbm, hbm, hbm],
        out_specs=(vmem, vmem),
        scratch_shapes=[
            pltpu.SMEM((3, 8, 128), jnp.int32),
            pltpu.VMEM((3, 8, 128), jnp.int32),
            pltpu.VMEM((KNN, 128), jnp.int32),
            pltpu.VMEM((128, 1536), half),
            pltpu.VMEM((1536, 384), half),
            pltpu.VMEM((128, 1536), half),
            pltpu.VMEM((512, 1536), half),
            pltpu.VMEM((128, 384), half),
            pltpu.VMEM((384, 128), half),
            pltpu.VMEM((128, 128), full),
            pltpu.VMEM((128, 384), full),
            pltpu.VMEM((768, 768), half),
            pltpu.VMEM((128, 128), half),
            pltpu.VMEM((3, 512, 768), half),
            pltpu.VMEM((3, 16, 32, 128), half),
        ]
        + [pltpu.VMEM((128, 16, 128), half)] * 3
        + [
            pltpu.VMEM((3, RING, 16, WAVE * 128), half),
            pltpu.VMEM((3, RING, 16, (KNN - WAVE) * 128), half),
            pltpu.VMEM((1536, WAVE * 128), half),
            pltpu.VMEM((1536, (KNN - WAVE) * 128), half),
            pltpu.VMEM((1536, 128), half),
            pltpu.VMEM((512, WAVE * 128), full),
            pltpu.VMEM((512, (KNN - WAVE) * 128), full),
            pltpu.VMEM((768, 384), full),
            pltpu.VMEM((1544, 384), full),
            pltpu.VMEM((RING, 24, 384), half),
            pltpu.VMEM((3, RING, 24, 128), half),
            pltpu.VMEM((3, 8, 64, 128), half),
            pltpu.VMEM((3, 8, 64, 128), half),
        ]
        + [pltpu.VMEM((2, a, 4, b, 16, 128), half) for a, b in SPLIT]
        + [pltpu.VMEM((a, 4, b, 16, 128), half) for a, b in SPLIT] * 2
        + [pltpu.VMEM((4, a, b, 16, 128), half) for a, b in SPLIT]
        + [pltpu.VMEM((3, 16, 24, 128), half)] * 2
        + [pltpu.SemaphoreType.DMA((4,)), pltpu.SemaphoreType.DMA((6,))]
        + [pltpu.SemaphoreType.DMA((3,))] * 18,
        compiler_params=pltpu.CompilerParams(
            collective_id=0, has_side_effects=True, vmem_limit_bytes=(65536 - 10752) * 1024
        ),
    )(jnp.transpose(neighbours), teacher, head_weight)


def solution(mesh):
    return jax.shard_map(
        body,
        mesh=mesh,
        in_specs=(P("dp", None, None), P(), P()),
        out_specs=(P("dp", None), P("dp", None, None)),
        check_vma=False,
    )
```

```python
import jax
import jax.numpy as jnp
from jax import lax
from jax.experimental import pallas as pl
from jax.experimental.pallas import tpu as pltpu
from jax.sharding import PartitionSpec as P

EPS = 1e-06
LOSS_SCALE = 128.0
SHIFT_SELF = 0.18
WEIGHT_SELF = 0.1
SHIFT_PAIR = 0.12
WEIGHT_PAIR = 0.5
MESH = pl.DeviceIdType.MESH
SIDE = 4
RING = 32
KNN = 6


def place(orient, index):
    y, x, z, c = index >> 5, (index >> 3) & 3, (index >> 1) & 3, index & 1
    if orient == 0:
        return y, index & 31
    if orient == 1:
        return x, (y << 3) + (index & 7)
    return z, ((index >> 3) << 1) + c


def device_at(orient, layer, spot):
    if orient == 0:
        return (layer << 5) + spot
    if orient == 1:
        return ((spot >> 3) << 5) + (layer << 3) + (spot & 7)
    return ((spot >> 1) << 3) + (layer << 1) + (spot & 1)


def shifted(spot, step):
    a = ((spot >> 3) + (step >> 3)) & 3
    b = ((spot >> 1) + (step >> 1)) & 3
    return (a << 3) + (b << 1) + ((spot + step) & 1)


def remote(src, dst, send, recv, device):
    return pltpu.make_async_remote_copy(
        src_ref=src, dst_ref=dst, send_sem=send, recv_sem=recv, device_id=(device,), device_id_type=MESH
    )


def unit_rows(values):
    total = jnp.sum(values * values, axis=-1, keepdims=True)
    return (values * lax.rsqrt(total + EPS)).astype(jnp.bfloat16)


def code_rows(codes):
    values = codes.astype(jnp.bfloat16).astype(jnp.float32)
    inverse = lax.rsqrt(jnp.sum(values * values, axis=-1, keepdims=True) + EPS)
    return (values * inverse).astype(jnp.bfloat16), inverse


def back_norm(grad, code_unit, inverse):
    values = code_unit.astype(jnp.float32)
    return (grad - values * jnp.sum(values * grad, axis=-1, keepdims=True)) * inverse


def dot(a, b, dims=((1,), (0,))):
    return lax.dot_general(a, b, (dims, ((), ())), preferred_element_type=jnp.float32)


def digit_sum(place_sum, step):
    return ((((place_sum >> 2) + (step >> 2)) & 3) << 2) + ((place_sum + step) & 3)


WAVE = 4
FAR1 = sorted(range(1, 16), key=lambda step: -(min(step >> 2, 4 - (step >> 2)) + min(step & 3, 4 - (step & 3))))
FAR2 = sorted(range(1, 32), key=lambda step: -(min(step >> 3, 4 - (step >> 3)) + min((step >> 1) & 3, 4 - ((step >> 1) & 3))))
SPLIT = ((1, 16), (4, 4), (16, 1))
GREETED = [(0, step) for step in range(1, 32)] + [(1, step) for step in range(8, 32)]
GREETED += [(2, step) for step in range(8, 32) if (step >> 1) & 3]
GREETED.sort(key=lambda at: -(min(at[1] >> 3, 4 - (at[1] >> 3)) + min((at[1] >> 1) & 3, 4 - ((at[1] >> 1) & 3))))


def step_kernel(
    nb_hbm, teacher_hbm, weight_hbm, head_ref, grad_ref,
    table_ref, tablev_ref, nbv_ref, teacher_ref, weight_ref, unit_ref, both_ref, code_ref, tcode_ref, inv_ref, self_ref,
    perm_ref, swap_ref, member_ref, stage, held0, held1, held2, picked0, picked1, wide0, wide1, tall_ref, product0, product1,
    mixed_ref, share_ref,
    cross_out, cross_in, part_out, part_in,
    out0, out1, out2, mid0, mid1, mid2, sum0, sum1, sum2, in0, in1, in2, tail_out, tail_in,
    load_sem, own_sem, *sems,
):
    held, share_out, share_mid = (held0, held1, held2), (out0, out1, out2), (mid0, mid1, mid2)
    share_sum, layer_in = (sum0, sum1, sum2), (in0, in1, in2)
    pairs = [(sems[2 * i], sems[2 * i + 1]) for i in range(len(sems) // 2)]
    deal_sem, layer_sem, serve0_sem, serve1_sem, cross_sem, part_sem, core_sem, axis_sem, tail_sem = pairs
    waves = (
        (0, WAVE, picked0, wide0, product0, serve0_sem),
        (WAVE, KNN, picked1, wide1, product1, serve1_sem),
    )
    me = lax.axis_index("dp")
    where = [place(o, me) for o in range(3)]
    core = me & 1
    barrier = pltpu.get_barrier_semaphore()
    loads = [
        pltpu.make_async_copy(teacher_hbm.at[0], teacher_ref, load_sem.at[0]),
        pltpu.make_async_copy(weight_hbm, weight_ref, load_sem.at[1]),
        pltpu.make_async_copy(nb_hbm, nbv_ref, load_sem.at[2]),
    ]
    for load in loads:
        load.start()

    for o, step in GREETED:
        layer, spot = where[o]
        pl.semaphore_signal(barrier, inc=1, device_id=(device_at(o, layer, shifted(spot, step)),), device_id_type=MESH)
    loads[0].wait()
    values = unit_rows(teacher_ref[...].astype(jnp.float32))
    unit_ref[...] = values
    tall_ref[...] = jnp.transpose(values.astype(jnp.float32)).astype(jnp.bfloat16)
    for load in loads[1:]:
        load.wait()
    named = nbv_ref[...]
    for o in range(3):
        up, at = place(o, named)
        tablev_ref[o, 0:KNN, :] = (up << 5) + ((at & 1) << 4) + (at >> 1)
        tablev_ref[o, KNN:8, :] = jnp.zeros((2, 128), jnp.int32)
    table_load = pltpu.make_async_copy(tablev_ref, table_ref, load_sem.at[3])
    table_load.start()
    table_load.wait()
    pl.semaphore_wait(barrier, len(GREETED))

    def tile(o, at):
        return tall_ref.at[pl.ds(pl.multiple_of(512 * o + at * 32, 32), 32)]

    own = []
    for o in range(3):
        layer, spot = where[o]
        at = spot >> 1

        def deal(step, carry):
            to = digit_sum(at, step)
            remote(
                tile(o, to), stage.at[o, at], deal_sem[0].at[o], deal_sem[1].at[o],
                device_at(o, layer, (to << 1) + core),
            ).start()
            return carry

        for step in FAR1:
            deal(step, 0)
        own.append(pltpu.make_async_copy(tile(o, at), stage.at[o, at], own_sem.at[o]))
        own[o].start()

    code_unit, inverse = code_rows(dot(unit_ref[...], weight_ref[...]))
    code_ref[...] = code_unit
    inv_ref[...] = jnp.broadcast_to(inverse, inv_ref.shape)

    for o in range(3):
        layer, spot = where[o]
        own[o].wait()
        part = stage.at[o, pl.ds(0, 15)]
        remote(part, part, deal_sem[0].at[o], deal_sem[1].at[o], me).wait()
        mine = held[o].at[pl.ds((layer * 2 + core) * 16, 16)]
        for hop in (4, 5, 2, 3, 6, 7, 1):
            up, side = (layer + (hop >> 1)) & 3, (core + hop) & 1
            remote(
                stage.at[o, :, pl.ds(pl.multiple_of(side * 16, 16), 16)], mine, layer_sem[0].at[o], layer_sem[1].at[o],
                device_at(o, up, spot - core + side),
            ).start()
        own[o] = pltpu.make_async_copy(stage.at[o, :, pl.ds(pl.multiple_of(core * 16, 16), 16)], mine, own_sem.at[o])
        own[o].start()

    units, codes = unit_ref[...], code_ref[...]
    tcorr = dot(units, units, ((1,), (1,)))
    scor = dot(codes, codes, ((1,), (1,)))
    gate = (-(LOSS_SCALE * WEIGHT_SELF) * (tcorr - SHIFT_SELF) * jnp.maximum(scor, 0.0)).astype(jnp.bfloat16)
    self_ref[...] = dot(gate, codes) + dot(gate, codes, ((0,), (0,)))

    both_ref[0:384, :] = jnp.transpose(weight_ref[...].astype(jnp.float32)).astype(jnp.bfloat16)
    both_ref[384:512, :] = units
    tcode_ref[...] = jnp.transpose(codes.astype(jnp.float32)).astype(jnp.bfloat16)
    row = lax.broadcasted_iota(jnp.int32, (768, 128), 0)
    col = lax.broadcasted_iota(jnp.int32, (768, 128), 1)
    block = (row * 2731) >> 16
    within = jnp.where(block == (col >> 2), row - 24 * block - (col & 3), -1)
    for k in range(KNN):
        perm_ref[:, 128 * k : 128 * (k + 1)] = jnp.where(within == 4 * k, 1.0, 0.0).astype(jnp.bfloat16)
    row = lax.broadcasted_iota(jnp.int32, (128, 128), 0)
    col = lax.broadcasted_iota(jnp.int32, (128, 128), 1)
    swap_ref[...] = jnp.where(
        col == (((row >> 2) & 1) << 6) + ((row >> 3) << 2) + (row & 3), 1.0, 0.0
    ).astype(jnp.bfloat16)

    spans = []
    for o in range(3):
        layer, spot = where[o]
        own[o].wait()
        part = held[o].at[pl.ds(0, 7 * 16)]
        remote(part, part, layer_sem[0].at[o], layer_sem[1].at[o], me).wait()
        spans.append(pl.ds(pl.multiple_of(512 * o + spot * 16, 16), 16))

    for first, last, picked, wide, _, sem in waves:

        def pick(o, step):
            layer, spot = where[o]
            asker = device_at(o, layer, shifted(spot, step))
            for k in range(first, last):
                lanes = slice(128 * (k - first), 128 * (k - first + 1))
                picked[o, step, :, lanes] = held[o][table_ref[o, k, asker]]
            return asker

        def serve(step, carry):
            for o in range(3):
                asker = pick(o, step)
                remote(picked.at[o, step], wide.at[spans[o]], sem[0].at[o], sem[1].at[o], asker).start()
            return carry

        lax.fori_loop(20, RING, serve, 0)
        lax.fori_loop(1, 20, serve, 0)
        for o in range(3):
            pick(o, 0)
            pltpu.make_async_copy(picked.at[o, 0], wide.at[spans[o]], own_sem.at[o + (3 if first else 0)]).start()

    slots = nbv_ref[...].astype(jnp.float32).astype(jnp.bfloat16)
    col = lax.broadcasted_iota(jnp.int32, (1, 768), 1)
    source = (col * 2731) >> 16
    slot_of = (col - 24 * source) >> 2
    mine = lax.broadcasted_iota(jnp.int32, (KNN, 768), 0) == slot_of
    image = lax.broadcasted_iota(jnp.int32, (128, 768), 0)
    row = lax.broadcasted_iota(jnp.int32, (512, 128), 0)
    same = (row & 3) == (lax.broadcasted_iota(jnp.int32, (512, 128), 1) & 3)
    for o in range(3):
        layer, spot = where[o]
        chosen = jnp.where(image == device_at(o, layer, source), 1.0, 0.0).astype(jnp.bfloat16)
        named = jnp.sum(jnp.where(mine, dot(slots, chosen), 0.0), axis=0, keepdims=True)
        owner = device_at(o, row >> 7, (((row >> 2) & 15) << 1) + ((row >> 6) & 1))
        owner = jnp.where(same, owner, -1).astype(jnp.float32)
        for k in range(KNN):
            lanes = slice(128 * k, 128 * (k + 1))
            member_ref[o, :, lanes] = jnp.where(owner == named[:, lanes], 1.0, 0.0).astype(jnp.bfloat16)

    for first, last, picked, wide, product_ref, sem in waves:
        for o in range(3):
            pltpu.make_async_copy(picked.at[o, 0], picked.at[o, 0], own_sem.at[o + (3 if first else 0)]).wait()
            part = picked.at[o, pl.ds(1, RING - 1)]
            remote(part, part, sem[0].at[o], sem[1].at[o], me).wait()
            third = slice(512 * o, 512 * (o + 1))
            product = dot(both_ref[:, third], wide[third, :])
            product_ref[...] = product if o == 0 else product_ref[...] + product

        values = product_ref[0:384, :].astype(jnp.bfloat16).astype(jnp.float32)
        partner_inv = lax.rsqrt(jnp.sum(values * values, axis=0, keepdims=True) + EPS)
        partner_code = (values * partner_inv).astype(jnp.bfloat16)
        tcorr = product_ref[384:512, :]
        scor = dot(code_ref[...], partner_code)
        gate = (-(LOSS_SCALE * WEIGHT_PAIR) * (tcorr - SHIFT_PAIR) * jnp.maximum(scor, 0.0)).astype(jnp.bfloat16)
        raw = dot(tcode_ref[...], gate)
        values = partner_code.astype(jnp.float32)
        cross = ((raw - values * jnp.sum(values * raw, axis=0, keepdims=True)) * partner_inv).astype(jnp.bfloat16)
        mixed = dot(perm_ref[:, 128 * first : 128 * last], cross, ((1,), (1,)))
        if first == 0:
            mixed_ref[...] = mixed
            self_ref[...] = self_ref[...] + dot(gate, partner_code, ((1,), (1,)))
            share_ref[0:1536, :] = dot(wide[...], cross, ((1,), (1,)))
        else:
            cross_out[...] = (mixed_ref[...] + mixed).reshape(RING, 24, 384).astype(jnp.bfloat16)

    def give(step, carry):
        for o in range(3):
            layer, spot = where[o]
            target = shifted(spot, step)
            remote(
                cross_out.at[target, :, pl.ds(128 * o, 128)], cross_in.at[o, spot], cross_sem[0].at[o], cross_sem[1].at[o],
                device_at(o, layer, target),
            ).start()
        return carry

    for step in FAR2:
        give(step, 0)
    for o in range(3):
        spot = where[o][1]
        cross_in[o, spot] = cross_out[spot, :, 128 * o : 128 * (o + 1)]

    grad = self_ref[...] + dot(gate, partner_code, ((1,), (1,)))
    own_grad = back_norm(grad, code_ref[...], inv_ref[:, 0:1])
    self_ref[...] = own_grad

    coarse = own_grad.astype(jnp.bfloat16)
    fine = (own_grad - coarse.astype(jnp.float32)).astype(jnp.bfloat16)
    share_ref[0:1536, :] = share_ref[0:1536, :] + (
        dot(wide1[...], cross, ((1,), (1,))) + dot(tall_ref[...], coarse) + dot(tall_ref[...], fine)
    )

    def cut_side(o, side):
        lanes = slice(128 * o, 128 * (o + 1))

        def cut(chip, carry):
            a, b, c = ((0, chip >> 4, chip & 15), (chip >> 4, (chip >> 2) & 3, chip & 3), (chip >> 2, chip & 3, 0))[o]
            rows = share_ref[pl.ds(pl.multiple_of(chip * 24, 8), 32), lanes]
            share_out[o][side, a, b, c] = jnp.where(side == 0, rows[0:16], rows[12:28]).astype(jnp.bfloat16)
            return carry

        lax.fori_loop(0, 64, cut, 0, unroll=4)

    for o in range(3):
        cut_side(o, 1 - core)
        remote(share_out[o].at[1 - core], share_mid[o], core_sem[0].at[o], core_sem[1].at[o], me + 1 - 2 * core).start()
    for o in range(3):
        cut_side(o, core)

    for o in range(3):
        layer, spot = where[o]
        remote(share_out[o].at[0], share_mid[o], core_sem[0].at[o], core_sem[1].at[o], me).wait()
        total = share_out[o][core].astype(jnp.float32) + share_mid[o][...].astype(jnp.float32)
        share_sum[o][...] = total.astype(jnp.bfloat16)
        for hop in (2, 1, 3):
            to = (layer + hop) & 3
            remote(
                share_sum[o].at[:, to], layer_in[o].at[layer], axis_sem[0].at[o], axis_sem[1].at[o], device_at(o, to, spot)
            ).start()
        layer_in[o][layer] = share_sum[o][:, layer]

    for o in range(3):
        layer, spot = where[o]
        part = cross_in.at[o, pl.ds(0, RING - 1)]
        remote(part, part, cross_sem[0].at[o], cross_sem[1].at[o], me).wait()
        piece = dot(member_ref[o], cross_in[o].reshape(768, 128))
        part_out[o] = piece.astype(jnp.bfloat16).reshape(8, 64, 128)
        mine = layer * 2 + core
        for hop in (4, 5, 2, 3, 6, 7, 1):
            up, side = (layer + (hop >> 1)) & 3, (core + hop) & 1
            remote(
                part_out.at[o, up * 2 + side], part_in.at[o, mine], part_sem[0].at[o], part_sem[1].at[o],
                device_at(o, up, spot - core + side),
            ).start()
        part_in[o, mine] = part_out[o, mine]

    for o in range(3):
        layer, spot = where[o]
        at = spot >> 1
        part = part_in.at[o, pl.ds(0, 7)]
        remote(part, part, part_sem[0].at[o], part_sem[1].at[o], me).wait()
        relayed = jnp.sum(part_in[o].reshape(4, 128, 128).astype(jnp.float32), axis=0).astype(jnp.bfloat16)
        tail_out[o, :, 16:24] = dot(swap_ref[...], relayed).reshape(16, 8, 128).astype(jnp.bfloat16)
        part = layer_in[o].at[pl.ds(0, SIDE - 1)]
        remote(part, part, axis_sem[0].at[o], axis_sem[1].at[o], me).wait()
        total = jnp.sum(layer_in[o][...].astype(jnp.float32), axis=0)
        tail_out[o, :, 0:16] = total.astype(jnp.bfloat16).reshape(16, 16, 128)

        def finish(step, carry):
            to = digit_sum(at, step)
            remote(
                tail_out.at[o, to], tail_in.at[o, at], tail_sem[0].at[o], tail_sem[1].at[o],
                device_at(o, layer, (to << 1) + core),
            ).start()
            return carry

        for step in FAR1:
            finish(step, 0)
        tail_in[o, at] = tail_out[o, at]

    for o in range(3):
        lanes = slice(128 * o, 128 * (o + 1))
        part = tail_in.at[o, pl.ds(0, 15)]
        remote(part, part, tail_sem[0].at[o], tail_sem[1].at[o], me).wait()
        relayed = tail_in[o, :, 16:24].astype(jnp.float32).reshape(128, 128)
        grad_ref[0, :, lanes] = self_ref[:, lanes] + relayed
        total = jnp.sum(tail_in[o, :, 0:16].astype(jnp.float32), axis=0)
        head_ref[:, lanes] = total[0:12]


def body(teacher, head_weight, neighbours):
    vmem = pl.BlockSpec(memory_space=pltpu.VMEM)
    hbm = pl.BlockSpec(memory_space=pl.ANY)
    half, full = jnp.bfloat16, jnp.float32
    return pl.pallas_call(
        step_kernel,
        out_shape=(jax.ShapeDtypeStruct((12, 384), full), jax.ShapeDtypeStruct((1, 128, 384), full)),
        in_specs=[hbm, hbm, hbm],
        out_specs=(vmem, vmem),
        scratch_shapes=[
            pltpu.SMEM((3, 8, 128), jnp.int32),
            pltpu.VMEM((3, 8, 128), jnp.int32),
            pltpu.VMEM((KNN, 128), jnp.int32),
            pltpu.VMEM((128, 1536), half),
            pltpu.VMEM((1536, 384), half),
            pltpu.VMEM((128, 1536), half),
            pltpu.VMEM((512, 1536), half),
            pltpu.VMEM((128, 384), half),
            pltpu.VMEM((384, 128), half),
            pltpu.VMEM((128, 128), full),
            pltpu.VMEM((128, 384), full),
            pltpu.VMEM((768, 768), half),
            pltpu.VMEM((128, 128), half),
            pltpu.VMEM((3, 512, 768), half),
            pltpu.VMEM((3, 16, 32, 128), half),
        ]
        + [pltpu.VMEM((128, 16, 128), half)] * 3
        + [
            pltpu.VMEM((3, RING, 16, WAVE * 128), half),
            pltpu.VMEM((3, RING, 16, (KNN - WAVE) * 128), half),
            pltpu.VMEM((1536, WAVE * 128), half),
            pltpu.VMEM((1536, (KNN - WAVE) * 128), half),
            pltpu.VMEM((1536, 128), half),
            pltpu.VMEM((512, WAVE * 128), full),
            pltpu.VMEM((512, (KNN - WAVE) * 128), full),
            pltpu.VMEM((768, 384), full),
            pltpu.VMEM((1544, 384), full),
            pltpu.VMEM((RING, 24, 384), half),
            pltpu.VMEM((3, RING, 24, 128), half),
            pltpu.VMEM((3, 8, 64, 128), half),
            pltpu.VMEM((3, 8, 64, 128), half),
        ]
        + [pltpu.VMEM((2, a, 4, b, 16, 128), half) for a, b in SPLIT]
        + [pltpu.VMEM((a, 4, b, 16, 128), half) for a, b in SPLIT] * 2
        + [pltpu.VMEM((4, a, b, 16, 128), half) for a, b in SPLIT]
        + [pltpu.VMEM((3, 16, 24, 128), half)] * 2
        + [pltpu.SemaphoreType.DMA((4,)), pltpu.SemaphoreType.DMA((6,))]
        + [pltpu.SemaphoreType.DMA((3,))] * 18,
        compiler_params=pltpu.CompilerParams(
            collective_id=0, has_side_effects=True, vmem_limit_bytes=(65536 - 10752) * 1024
        ),
    )(jnp.transpose(neighbours), teacher, head_weight)


def solution(mesh):
    return jax.shard_map(
        body,
        mesh=mesh,
        in_specs=(P("dp", None, None), P(), P()),
        out_specs=(P("dp", None), P("dp", None, None)),
        check_vma=False,
    )
```
